256 devices in a mesh: ax: 16 (over z, core), xs: 16 (over y, x).
Axes of the slice: x: 4, y: 4, z: 8, core: 2. Of those that a mesh axis runs over, the one named last changes fastest.
Arguments:
- populations: float32 [19, 64, 256, 256], P(None, 'ax', 'xs'), may hold values from 0 to 1, as said below
- solute: float32 [2, 7, 64, 256, 256], P(None, None, 'ax', 'xs'), may hold values from 0 to 1, as said below
- adsorbed: float32 [2, 64, 256, 256], P(None, 'ax', 'xs'), may hold values from 0 to 0.05
- capacity: float32 [64, 256, 256], P('ax', 'xs'), may hold values from 0.1 to 1
- solid: int32 [64, 256, 256], P('ax', 'xs'), may hold values 0 or 1
Outputs:
- populations_out: float32 [19, 64, 256, 256], P(None, 'ax', 'xs')
- solute_out: float32 [2, 7, 64, 256, 256], P(None, None, 'ax', 'xs')
- adsorbed_out: float32 [2, 64, 256, 256], P(None, 'ax', 'xs')
The draws below stay inside these ranges and needn't reach their ends.
Inputs may be any that keep to these rules, and one draw needn't show every extreme that they name: `populations`: every entry is positive. `solute`: every entry is positive.
All inputs are finite; a program needn't handle non-finite values. No bound on the sum of `solid` on one device may be relied on, other than what follows from the above.
Results may differ from the reference program's by a relative error of at most 0.0001.
Values sent between devices are 32-bit elements; how exact they have to be, the bound alone decides.
No kernel may reach another device: no remote copies, remote signals or barrier semaphores. Data moves between devices by JAX's collectives and lax.ppermute only.
A program may use at most 64 MiB of HBM per device.

```python
import math
import jax
import jax.numpy as jnp
import numpy as np
from jax import lax

STEPS = 4
NZ = 64
NX = 256
NY = 256


AXIAL_FLOW = np.array([0, 1, -1, 0, 0, 0, 0, 1, -1, 1, -1, 1, -1, 1, -1, 0, 0, 0, 0])


LATTICE_WEIGHTS = np.array([1.0 / 3.0] + [1.0 / 18.0] * 6 + [1.0 / 36.0] * 12)


SOLUTE_WEIGHTS = np.array([0.25] + [0.125] * 6)


def draw_populations(key, part):
    key = jax.random.fold_in(key, 11)
    shape = (19, NZ, NX, NY)
    factor = 1.0 + 0.15 * jax.random.truncated_normal(key, -3.0, 3.0, shape, jnp.float32)
    weights = jnp.asarray(LATTICE_WEIGHTS, jnp.float32)[:, None, None, None]
    lift = 1.0 + 0.15 * jnp.asarray(AXIAL_FLOW, jnp.float32)[:, None, None, None]
    return weights * lift * factor


def draw_solute(key, part):
    key = jax.random.fold_in(key, 12)
    level_key, noise_key = jax.random.split(key)
    shape = (2, 7, NZ, NX, NY)
    level = jnp.exp(jax.random.uniform(level_key, (2, 1, NZ, NX, NY), jnp.float32, jnp.log(0.2), jnp.log(2.0)))
    factor = 1.0 + 0.15 * jax.random.truncated_normal(noise_key, -3.0, 3.0, shape, jnp.float32)
    weights = jnp.asarray(SOLUTE_WEIGHTS, jnp.float32)[None, :, None, None, None]
    return weights * level * factor


def with_ends(drawn, rng, smallest, largest):
    spot = [jax.random.randint(jax.random.fold_in(rng, axis), (), 0, length) for axis, length in enumerate(drawn.shape)]
    main_axis = drawn.shape.index(max(drawn.shape))
    beside = spot[:main_axis] + [(spot[main_axis] + 1) % drawn.shape[main_axis]] + spot[main_axis + 1:]
    return drawn.at[tuple(spot)].set(smallest).at[tuple(beside)].set(largest)


def block_scale(rng, extent, cuts, smallest, largest):
    gain = 1.0
    for position, parts in cuts:
        heights = jax.random.uniform(jax.random.fold_in(jax.random.fold_in(rng, 6), position), (parts,), jnp.float32, smallest / len(cuts), largest / len(cuts))
        gain = gain * jnp.repeat(jnp.exp(heights), extent[position] // parts).reshape((-1,) + (1,) * (len(extent) - 1 - position))
    return gain


def setup_inputs(seed: int = 0) -> dict:
    arg_keys = jax.random.split(jax.random.key(seed), 6)
    return {
        "populations": draw_populations(jax.random.fold_in(arg_keys[5], 71), 0),
        "solute": draw_solute(jax.random.fold_in(arg_keys[5], 71), 0),
        "adsorbed": jnp.clip(0.05 * jax.random.uniform(arg_keys[2], (2, NZ, NX, NY), jnp.float32) ** block_scale(arg_keys[2], (2, NZ, NX, NY), ((1, 16), (2, 16)), -0.2, 0.2), 0.0, 0.05),
        "capacity": jnp.clip(jnp.exp(math.log(1.0) - 2.3025851 * jax.random.uniform(arg_keys[3], (NZ, NX, NY), jnp.float32) ** block_scale(arg_keys[3], (NZ, NX, NY), ((0, 16), (1, 16)), -0.2, 0.2)), 0.1, 1.0),
        "solid": with_ends((jax.random.randint(arg_keys[4], (NZ, NX, NY), 0, 5) < 3).astype(jnp.int32), jax.random.fold_in(arg_keys[4], 1), 0, 1),
    }


VELOCITY = np.array([[0, 0, 0], [1, 0, 0], [-1, 0, 0], [0, 1, 0], [0, -1, 0], [0, 0, 1], [0, 0, -1],
                     [1, 1, 0], [-1, -1, 0], [1, -1, 0], [-1, 1, 0], [1, 0, 1], [-1, 0, -1], [1, 0, -1],
                     [-1, 0, 1], [0, 1, 1], [0, -1, -1], [0, 1, -1], [0, -1, 1]])
REVERSE = np.array([0, 2, 1, 4, 3, 6, 5, 8, 7, 10, 9, 12, 11, 14, 13, 16, 15, 18, 17])
WEIGHT_FLOW = np.array([1.0 / 3.0] + [1.0 / 18.0] * 6 + [1.0 / 36.0] * 12)
WEIGHT_SOLUTE = np.array([0.25] + [0.125] * 6)
OMEGA_SOLUTE = np.array([1.0, 0.7])
ON_RATE = np.array([0.5, 0.2])
OFF_RATE = np.array([0.05, 0.1])


def collide(pops, solute, adsorbed, capacity, solid):
    wetted = solid == 0
    table = jnp.asarray(VELOCITY, jnp.float32)
    weights = jnp.asarray(WEIGHT_FLOW, jnp.float32)[:, None, None, None]
    density = jnp.sum(pops, axis=0)
    momentum = jnp.tensordot(table.T, pops, axes=1, precision=lax.Precision.HIGHEST)
    velocity = momentum / density
    projection = jnp.tensordot(table, velocity, axes=1, precision=lax.Precision.HIGHEST)
    speed_square = jnp.sum(velocity * velocity, axis=0)
    balance = weights * density * (1.0 + 3.0 * projection + 4.5 * projection * projection - 1.5 * speed_square)
    reversed_pops = pops[REVERSE]
    balance_back = balance[REVERSE]
    forcing = 3.0 * weights * density * table[:, 0][:, None, None, None] * 0.001
    relaxed = (pops - 1.25 * 0.5 * ((pops + reversed_pops) - (balance + balance_back))
               - 0.75 * 0.5 * ((pops - reversed_pops) - (balance - balance_back)) + forcing)
    flow_out = jnp.where(wetted, relaxed, reversed_pops)
    small_table = table[:7]
    small_weights = jnp.asarray(WEIGHT_SOLUTE, jnp.float32)[None, :, None, None, None]
    concentration = jnp.sum(solute, axis=1)
    advective = jnp.tensordot(small_table, velocity, axes=1, precision=lax.Precision.HIGHEST)
    solute_balance = small_weights * concentration[:, None] * (1.0 + 4.0 * advective[None])
    occupied = adsorbed[0] + adsorbed[1]
    on_rate = jnp.asarray(ON_RATE, jnp.float32)[:, None, None, None]
    off_rate = jnp.asarray(OFF_RATE, jnp.float32)[:, None, None, None]
    uptake = jnp.where(wetted, on_rate * concentration * (capacity - occupied) - off_rate * adsorbed, 0.0)
    bound_next = adsorbed + uptake
    omega = jnp.asarray(OMEGA_SOLUTE, jnp.float32)[:, None, None, None, None]
    solute_relaxed = solute - omega * (solute - solute_balance) - small_weights * uptake[:, None]
    solute_next = jnp.where(wetted, solute_relaxed, solute[:, REVERSE[:7]])
    return flow_out, solute_next, bound_next


def moved(field, direction):
    shift_amounts = tuple(int(value) for value in VELOCITY[direction])
    return jnp.roll(field, shift_amounts, axis=(0, 1, 2))


def reference(populations, solute, adsorbed, capacity, solid):
    pops, species, bound = populations, solute, adsorbed
    for repeat in range(STEPS):
        flow_out, solute_next, bound = collide(pops, species, bound, capacity, solid)
        pops = jnp.stack([moved(flow_out[direction], direction) for direction in range(19)])
        species = jnp.stack([jnp.stack([moved(solute_next[kind, direction], direction) for direction in range(7)])
                             for kind in range(2)])
    return pops, species, bound
```

```python
import functools
import jax
import jax.numpy as jnp
import numpy as np
from jax import lax
from jax.experimental import pallas as pl
from jax.experimental.pallas import tpu as pltpu
from jax.sharding import PartitionSpec as P


STEPS = 4
DEPTH = 4
ROWS = 24
VELOCITY = np.array(
    [
        [0, 0, 0],
        [1, 0, 0],
        [-1, 0, 0],
        [0, 1, 0],
        [0, -1, 0],
        [0, 0, 1],
        [0, 0, -1],
        [1, 1, 0],
        [-1, -1, 0],
        [1, -1, 0],
        [-1, 1, 0],
        [1, 0, 1],
        [-1, 0, -1],
        [1, 0, -1],
        [-1, 0, 1],
        [0, 1, 1],
        [0, -1, -1],
        [0, 1, -1],
        [0, -1, 1],
    ]
)
ALL = [tuple(int(c) for c in v) for v in np.concatenate([VELOCITY, VELOCITY[:7], VELOCITY[:7]])]
FIELDS = len(ALL)
UP = [k for k in range(FIELDS) if ALL[k][0] == 1]
DOWN = [k for k in range(FIELDS) if ALL[k][0] == -1]
OMEGA_SOLUTE = (1.0, 0.7)
ON_RATE = (0.5, 0.2)
OFF_RATE = (0.05, 0.1)
VMEM = pl.BlockSpec(memory_space=pltpu.VMEM)


def rim_rows(k, side):
    return DEPTH - 1 + side * ALL[k][1]


def message_plan(side):
    plan, offset = [], 0
    for z in range(4):
        for k in range(FIELDS):
            n = rim_rows(k, side)
            plan.append(("r", k, z, n, offset))
            offset += n
        for name in ("a0", "a1", "c", "s"):
            plan.append((name, 0, z, DEPTH - 1, offset))
            offset += DEPTH - 1
    return plan, offset


MESSAGE = -(-message_plan(1)[1] // 8) * 8


def collide(f, adsorbed, capacity, fluid):
    out = [None] * FIELDS
    s = {k: f[k] + f[k + 1] for k in range(1, 19, 2)}
    d = {k: f[k] - f[k + 1] for k in range(1, 19, 2)}
    axis = s[1] + s[3] + s[5]
    edge = (s[7] + s[9]) + (s[11] + s[13]) + (s[15] + s[17])
    density = f[0] + axis + edge
    mz = d[1] + d[7] + d[9] + d[11] + d[13]
    mx = d[3] + d[7] - d[9] + d[15] + d[17]
    my = d[5] + d[11] - d[13] + d[15] - d[17]
    inverse = 1.0 / density
    uz, ux, uy = mz * inverse, mx * inverse, my * inverse
    base = 1.0 - 1.5 * (uz * uz + ux * ux + uy * uy)
    even = (1.25 / 36.0) * density
    rest_even = even * base
    square = 4.5 * even
    oz = (2.25 / 36.0) * mz + (0.003 / 36.0) * density
    ox = (2.25 / 36.0) * mx
    oy = (2.25 / 36.0) * my
    out[0] = jnp.where(fluid, 12.0 * rest_even - 0.25 * f[0], f[0])
    pairs = {
        1: (uz, oz), 3: (ux, ox), 5: (uy, oy),
        7: (uz + ux, oz + ox), 9: (uz - ux, oz - ox),
        11: (uz + uy, oz + oy), 13: (uz - uy, oz - oy),
        15: (ux + uy, ox + oy), 17: (ux - uy, ox - oy),
    }
    for k, (u, o) in pairs.items():
        e = rest_even + square * (u * u)
        if k < 7:
            e, o = e + e, o + o
        a = e - 0.125 * s[k]
        b = o + 0.125 * d[k]
        out[k] = jnp.where(fluid, a + b, f[k + 1])
        out[k + 1] = jnp.where(fluid, a - b, f[k])
    occupied = adsorbed[0] + adsorbed[1]
    free = capacity - occupied
    bound = []
    for kind in range(2):
        g = f[19 + 7 * kind: 26 + 7 * kind]
        total = g[0] + (g[1] + g[2]) + (g[3] + g[4]) + (g[5] + g[6])
        uptake = ON_RATE[kind] * total * free - OFF_RATE[kind] * adsorbed[kind]
        bound.append(jnp.where(fluid, adsorbed[kind] + uptake, adsorbed[kind]))
        omega = OMEGA_SOLUTE[kind]
        moved = total if omega == 1.0 else omega * total
        share = 0.125 * (moved - uptake)
        drift = 0.5 * moved

        def kept(h):
            return 0.0 if omega == 1.0 else (1.0 - omega) * h

        out[19 + 7 * kind] = jnp.where(fluid, kept(g[0]) + (share + share), g[0])
        for j, u in ((1, uz), (3, ux), (5, uy)):
            o = drift * u
            out[19 + 7 * kind + j] = jnp.where(fluid, kept(g[j]) + (share + o), g[j + 1])
            out[19 + 7 * kind + j + 1] = jnp.where(fluid, kept(g[j + 1]) + (share - o), g[j])
    return out, bound


def parity(axis):
    return lax.rem(lax.axis_index(axis), 2)


def first_kernel(pop, sol, ads, cap, solid, r_out, ads_out, xa, xb):
    for z in range(4):
        for r in range(0, 16, 8):
            for c in range(0, 256, 128):
                at = (z, slice(r, r + 8), slice(c, c + 128))
                f = [pop[(k,) + at] for k in range(19)]
                f += [sol[(s, k) + at] for s in range(2) for k in range(7)]
                out, bound = collide(
                    f, [ads[(0,) + at], ads[(1,) + at]], cap[at], solid[at] == 0
                )
                for k in range(FIELDS):
                    r_out[(k,) + at] = out[k]
                for s in range(2):
                    ads_out[(s,) + at] = bound[s]

    def pack(side, message):
        plan, used = message_plan(side)
        for name, k, z, n, offset in plan:
            rows = slice(16 - n, 16) if side == 1 else slice(0, n)
            if name == "r":
                piece = r_out[k, z, rows, :]
            elif name == "a0" or name == "a1":
                piece = ads_out[int(name[1]), z, rows, :]
            elif name == "c":
                piece = cap[z, rows, :]
            else:
                piece = solid[z, rows, :].astype(jnp.float32)
            message[offset:offset + n, :] = piece

    q = parity("xs")

    @pl.when(q == 0)
    def _():
        pack(1, xa)
        pack(-1, xb)

    @pl.when(q == 1)
    def _():
        pack(-1, xa)
        pack(1, xb)


def send_faces(read, za, zb):
    p = parity("ax")

    @pl.when(p == 0)
    def _():
        for i, k in enumerate(DOWN):
            zb[i] = read(k, 0)
        for i, k in enumerate(UP):
            za[i] = read(k, 3)

    @pl.when(p == 1)
    def _():
        for i, k in enumerate(UP):
            zb[i] = read(k, 3)
        for i, k in enumerate(DOWN):
            za[i] = read(k, 0)


def rim_kernel(r16, xa, xb, rim, rim_ads, rim_cap, rim_solid, za, zb):
    def unpack(side, message):
        plan, used = message_plan(side)
        for name, k, z, n, offset in plan:
            rows = slice(8 - n, 8) if side == 1 else slice(0, n)
            piece = message[offset:offset + n, :]
            if name == "r":
                rim[k, z, rows, :] = piece
            elif name == "a0" or name == "a1":
                rim_ads[int(name[1]), z, rows, :] = piece
            elif name == "c":
                rim_cap[z, rows, :] = piece
            else:
                rim_solid[z, rows, :] = piece

    q = parity("xs")

    @pl.when(q == 0)
    def _():
        unpack(-1, xa)
        unpack(1, xb)

    @pl.when(q == 1)
    def _():
        unpack(1, xa)
        unpack(-1, xb)

    send_faces(lambda k, z: jnp.concatenate([r16[k, z], rim[k, z]], axis=0), za, zb)


def arrive(k, z, whole, za, zb, p):
    cz, cx, cy = ALL[k]
    below = z - cz
    if below == -1:
        i = UP.index(k)
        v = jnp.where(p == 0, zb[i], za[i])
    elif below == 4:
        i = DOWN.index(k)
        v = jnp.where(p == 0, za[i], zb[i])
    else:
        v = whole(k, below)
    if cx:
        v = pltpu.roll(v, cx % ROWS, 0)
    if cy:
        v = pltpu.roll(v, cy % 256, 1)
    return v


def step_kernel(first, last, *refs):
    refs = list(refs)
    if first:
        r16, rim, ads16, rim_ads = refs[:4]
        refs = refs[4:]
    else:
        r24, ads24 = refs[:2]
        refs = refs[2:]
    cap, rim_cap, solid, rim_solid, za, zb = refs[:6]
    r_out, ads_out, za_out, zb_out, moved = refs[6:]
    p = parity("ax")

    def whole(k, z):
        if first:
            return jnp.concatenate([r16[k, z], rim[k, z]], axis=0)
        return r24[k, z]

    def block(main, side, at, r, c):
        cols = slice(c, c + 128)
        if r < 16:
            return main[at + (slice(r, r + 8), cols)]
        return side[at + (slice(0, 8), cols)]

    for z in range(4):
        through = [k for k in range(FIELDS) if ALL[k][1:] == (0, 0) and 0 <= z - ALL[k][0] < 4]
        for k in range(FIELDS):
            if k not in through:
                moved[k, z] = arrive(k, z, whole, za, zb, p)
        for r in range(0, ROWS, 8):
            for c in range(0, 256, 128):
                here = (slice(r, r + 8), slice(c, c + 128))
                f = []
                for k in range(FIELDS):
                    if k not in through:
                        f.append(moved[(k, z) + here])
                    elif first:
                        f.append(block(r16, rim, (k, z - ALL[k][0]), r, c))
                    else:
                        f.append(r24[(k, z - ALL[k][0]) + here])
                if first:
                    ads = [block(ads16, rim_ads, (s, z), r, c) for s in range(2)]
                else:
                    ads = [ads24[(s, z) + here] for s in range(2)]
                capacity = block(cap, rim_cap, (z,), r, c)
                if r < 16:
                    fluid = solid[(z,) + here] == 0
                else:
                    fluid = rim_solid[z, 0:8, c:c + 128] == 0.0
                out, bound = collide(f, ads, capacity, fluid)
                for k in range(FIELDS):
                    r_out[(k, z) + here] = out[k]
                if r < 16 or not last:
                    for s in range(2):
                        ads_out[(s, z) + here] = bound[s]
    send_faces(lambda k, z: r_out[k, z], za_out, zb_out)


def last_kernel(r24, za, zb, pop_out, sol_out):
    p = parity("ax")
    for z in range(4):
        for k in range(FIELDS):
            v = arrive(k, z, lambda kk, zz: r24[kk, zz], za, zb, p)[0:16]
            if k < 19:
                pop_out[k, z] = v
            else:
                sol_out[(k - 19) // 7, (k - 19) % 7, z] = v


def call(kernel, outs, args, scratch=(), limit=16 << 20):
    return pl.pallas_call(
        kernel,
        out_shape=[jax.ShapeDtypeStruct(s, jnp.float32) for s in outs],
        in_specs=[VMEM] * len(args),
        out_specs=[VMEM] * len(outs),
        scratch_shapes=list(scratch),
        compiler_params=pltpu.CompilerParams(vmem_limit_bytes=limit),
    )(*args)


def swaps(axis):
    count = lax.axis_size(axis)
    inner = [(i, i ^ 1) for i in range(count)]
    outer = [(i, (i + 1) % count if i % 2 else (i - 1) % count) for i in range(count)]
    return inner, outer


def body(populations, solute, adsorbed, capacity, solid):
    inner_z, outer_z = swaps("ax")
    inner_x, outer_x = swaps("xs")
    face = (7, ROWS, 256)
    r16, ads16, xa, xb = call(
        first_kernel,
        [(FIELDS, 4, 16, 256), (2, 4, 16, 256), (MESSAGE, 256), (MESSAGE, 256)],
        [populations, solute, adsorbed, capacity, solid],
    )
    xb = lax.ppermute(xb, "xs", outer_x)
    xa = lax.ppermute(xa, "xs", inner_x)
    rim, rim_ads, rim_cap, rim_solid, za, zb = call(
        rim_kernel,
        [(FIELDS, 4, 8, 256), (2, 4, 8, 256), (4, 8, 256), (4, 8, 256), face, face],
        [r16, xa, xb],
    )
    state = [r16, rim, ads16, rim_ads]
    for step in range(1, STEPS):
        zb = lax.ppermute(zb, "ax", outer_z)
        za = lax.ppermute(za, "ax", inner_z)
        last = step == STEPS - 1
        r24, ads, za, zb = call(
            functools.partial(step_kernel, step == 1, last),
            [(FIELDS, 4, ROWS, 256), (2, 4, 16 if last else ROWS, 256), face, face],
            state + [capacity, rim_cap, solid, rim_solid, za, zb],
            [pltpu.VMEM((FIELDS, 4, ROWS, 256), jnp.float32)],
        )
        state = [r24, ads]
    zb = lax.ppermute(zb, "ax", outer_z)
    za = lax.ppermute(za, "ax", inner_z)
    pops, species = call(
        last_kernel, [(19, 4, 16, 256), (2, 7, 4, 16, 256)], [r24, za, zb]
    )
    return pops, species, ads


def solution(mesh):
    placed = (
        P(None, "ax", "xs", None),
        P(None, None, "ax", "xs", None),
        P(None, "ax", "xs", None),
        P("ax", "xs", None),
        P("ax", "xs", None),
    )
    return jax.shard_map(
        body,
        mesh=mesh,
        in_specs=placed,
        out_specs=(
            P(None, "ax", "xs", None),
            P(None, None, "ax", "xs", None),
            P(None, "ax", "xs", None),
        ),
        check_vma=False,
    )
```

```python
import functools
import jax
import jax.numpy as jnp
import numpy as np
from jax import lax
from jax.experimental import pallas as pl
from jax.experimental.pallas import tpu as pltpu
from jax.sharding import PartitionSpec as P


STEPS = 4
DEPTH = 4
ROWS = 24
VELOCITY = np.array(
    [
        [0, 0, 0],
        [1, 0, 0],
        [-1, 0, 0],
        [0, 1, 0],
        [0, -1, 0],
        [0, 0, 1],
        [0, 0, -1],
        [1, 1, 0],
        [-1, -1, 0],
        [1, -1, 0],
        [-1, 1, 0],
        [1, 0, 1],
        [-1, 0, -1],
        [1, 0, -1],
        [-1, 0, 1],
        [0, 1, 1],
        [0, -1, -1],
        [0, 1, -1],
        [0, -1, 1],
    ]
)
ALL = [tuple(int(c) for c in v) for v in np.concatenate([VELOCITY, VELOCITY[:7], VELOCITY[:7]])]
FIELDS = len(ALL)
UP = [k for k in range(FIELDS) if ALL[k][0] == 1]
DOWN = [k for k in range(FIELDS) if ALL[k][0] == -1]
OMEGA_SOLUTE = (1.0, 0.7)
ON_RATE = (0.5, 0.2)
OFF_RATE = (0.05, 0.1)
VMEM = pl.BlockSpec(memory_space=pltpu.VMEM)
ANY = pl.BlockSpec(memory_space=pl.ANY)
HBM = pl.BlockSpec(memory_space=pltpu.HBM)
MIRROR = [
    19 * (k >= 19) + 7 * (k >= 26)
    + ALL[: 19 if k < 19 else 7].index((-ALL[k][0],) + ALL[k][1:])
    for k in range(FIELDS)
]


def rim_rows(k, side):
    return DEPTH - 1 + side * ALL[k][1]


def message_plan(side):
    plan, offset = [], 0
    for z in range(4):
        for k in range(FIELDS):
            n = rim_rows(k, side)
            plan.append(("r", k, z, n, offset))
            offset += n
        for name in ("a0", "a1", "c", "s"):
            plan.append((name, 0, z, DEPTH - 1, offset))
            offset += DEPTH - 1
    return plan, offset


MESSAGE = -(-message_plan(1)[1] // 8) * 8


def collide(f, adsorbed, capacity, fluid, push):
    out = [None] * FIELDS
    s = {k: f[k] + f[k + 1] for k in range(1, 19, 2)}
    d = {k: f[k] - f[k + 1] for k in range(1, 19, 2)}
    axis = s[1] + s[3] + s[5]
    edge = (s[7] + s[9]) + (s[11] + s[13]) + (s[15] + s[17])
    density = f[0] + axis + edge
    mz = d[1] + d[7] + d[9] + d[11] + d[13]
    mx = d[3] + d[7] - d[9] + d[15] + d[17]
    my = d[5] + d[11] - d[13] + d[15] - d[17]
    inverse = 1.0 / density
    uz, ux, uy = mz * inverse, mx * inverse, my * inverse
    base = 1.0 - 1.5 * (uz * uz + ux * ux + uy * uy)
    even = (1.25 / 36.0) * density
    rest_even = even * base
    square = 4.5 * even
    oz = (2.25 / 36.0) * mz + (push * (0.003 / 36.0)) * density
    ox = (2.25 / 36.0) * mx
    oy = (2.25 / 36.0) * my
    out[0] = jnp.where(fluid, 12.0 * rest_even - 0.25 * f[0], f[0])
    pairs = {
        1: (uz, oz), 3: (ux, ox), 5: (uy, oy),
        7: (uz + ux, oz + ox), 9: (uz - ux, oz - ox),
        11: (uz + uy, oz + oy), 13: (uz - uy, oz - oy),
        15: (ux + uy, ox + oy), 17: (ux - uy, ox - oy),
    }
    for k, (u, o) in pairs.items():
        e = rest_even + square * (u * u)
        if k < 7:
            e, o = e + e, o + o
        a = e - 0.125 * s[k]
        b = o + 0.125 * d[k]
        out[k] = jnp.where(fluid, a + b, f[k + 1])
        out[k + 1] = jnp.where(fluid, a - b, f[k])
    occupied = adsorbed[0] + adsorbed[1]
    free = capacity - occupied
    bound = []
    for kind in range(2):
        g = f[19 + 7 * kind: 26 + 7 * kind]
        total = g[0] + (g[1] + g[2]) + (g[3] + g[4]) + (g[5] + g[6])
        uptake = ON_RATE[kind] * total * free - OFF_RATE[kind] * adsorbed[kind]
        bound.append(jnp.where(fluid, adsorbed[kind] + uptake, adsorbed[kind]))
        omega = OMEGA_SOLUTE[kind]
        moved = total if omega == 1.0 else omega * total
        share = 0.125 * (moved - uptake)
        drift = 0.5 * moved

        def kept(h):
            return 0.0 if omega == 1.0 else (1.0 - omega) * h

        out[19 + 7 * kind] = jnp.where(fluid, kept(g[0]) + (share + share), g[0])
        for j, u in ((1, uz), (3, ux), (5, uy)):
            o = drift * u
            out[19 + 7 * kind + j] = jnp.where(fluid, kept(g[j]) + (share + o), g[j + 1])
            out[19 + 7 * kind + j + 1] = jnp.where(fluid, kept(g[j + 1]) + (share - o), g[j])
    return out, bound


def parity(axis):
    return lax.rem(lax.axis_index(axis), 2)


def turned(p, k):
    return jnp.where(p == 0, k, MIRROR[k]) if MIRROR[k] != k else k


def layer(p, j):
    return jnp.where(p == 0, j, 3 - j)


def first_kernel(
    pop, sol, ads, cap, solid, r_out, ads_out, cap_out, solid_out, xa, xb,
    pop_in, sol_in, ads_in, cap_in, solid_in, sems,
):
    p = parity("ax")
    push = jnp.where(p == 0, 1.0, -1.0)
    copies = []
    for j in range(4):
        z = layer(p, j)
        pairs = [
            (pop.at[:, z], pop_in.at[:, j]),
            (sol.at[:, :, z], sol_in.at[:, :, j]),
            (ads.at[:, z], ads_in.at[:, j]),
            (cap.at[z], cap_in.at[j]),
            (solid.at[z], solid_in.at[j]),
        ]
        copies.append([
            pltpu.make_async_copy(a, b, sems.at[j, i]) for i, (a, b) in enumerate(pairs)
        ])
    for group in copies:
        for copy in group:
            copy.start()
    for j in range(4):
        for copy in copies[j]:
            copy.wait()
        for r in range(0, 16, 8):
            for c in range(0, 256, 128):
                at = (j, slice(r, r + 8), slice(c, c + 128))
                f = [pop_in[(turned(p, k),) + at] for k in range(19)]
                f += [
                    sol_in[(s, turned(p, 19 + 7 * s + k) - 19 - 7 * s) + at]
                    for s in range(2) for k in range(7)
                ]
                cap_out[at] = cap_in[at]
                solid_out[at] = solid_in[at].astype(jnp.float32)
                out, bound = collide(
                    f, [ads_in[(0,) + at], ads_in[(1,) + at]], cap_in[at],
                    solid_in[at] == 0, push,
                )
                for k in range(FIELDS):
                    r_out[(k,) + at] = out[k]
                for s in range(2):
                    ads_out[(s,) + at] = bound[s]

    def pack(side, message):
        plan, used = message_plan(side)
        for name, k, j, n, offset in plan:
            rows = slice(16 - n, 16) if side == 1 else slice(0, n)
            source = {
                "r": lambda: r_out[k, j, rows, :],
                "a0": lambda: ads_out[0, j, rows, :],
                "a1": lambda: ads_out[1, j, rows, :],
                "c": lambda: cap_out[j, rows, :],
                "s": lambda: solid_out[j, rows, :],
            }
            message[offset:offset + n, :] = source[name]()

    q = parity("xs")

    @pl.when(q == 0)
    def _():
        pack(1, xa)
        pack(-1, xb)

    @pl.when(q == 1)
    def _():
        pack(-1, xa)
        pack(1, xb)


def shifted(k, v):
    cz, cx, cy = ALL[k]
    if cx:
        v = pltpu.roll(v, cx % ROWS, 0)
    if cy:
        v = pltpu.roll(v, cy % 256, 1)
    return v


def face_rows(edge):
    return -(-7 * (16 + 2 * edge) // 8) * 8


def send_face(fields, read, message, edge):
    for i, k in enumerate(fields):
        v = shifted(k, read(k))
        message[16 * i:16 * i + 16, :] = v[0:16]
        if edge:
            at = 112 + 2 * edge * i
            message[at:at + edge, :] = v[16:16 + edge]
            message[at + edge:at + 2 * edge, :] = v[24 - edge:24]


def receive_face(k, fields, message, edge, moved):
    i = fields.index(MIRROR[k])
    moved[0:16, :] = message[16 * i:16 * i + 16, :]
    if edge:
        at = 112 + 2 * edge * i
        moved[16:16 + edge, :] = message[at:at + edge, :]
        moved[24 - edge:24, :] = message[at + edge:at + 2 * edge, :]


def rim_kernel(r16, ads16, cap16, solid16, xa, xb, rim, ads, cap, solid, za, zb):
    for j in range(4):
        for s in range(2):
            ads[s, j, 0:16, :] = ads16[s, j]
        cap[j, 0:16, :] = cap16[j]
        solid[j, 0:16, :] = solid16[j]

    def unpack(side, message):
        plan, used = message_plan(side)
        for name, k, j, n, offset in plan:
            low = 8 - n if side == 1 else 0
            piece = message[offset:offset + n, :]
            if name == "r":
                rim[k, j, low:low + n, :] = piece
            else:
                rows = slice(16 + low, 16 + low + n)
                if name == "c":
                    cap[j, rows, :] = piece
                elif name == "s":
                    solid[j, rows, :] = piece
                else:
                    ads[int(name[1]), j, rows, :] = piece

    q = parity("xs")

    @pl.when(q == 0)
    def _():
        unpack(-1, xa)
        unpack(1, xb)

    @pl.when(q == 1)
    def _():
        unpack(1, xa)
        unpack(-1, xb)

    def read(j):
        return lambda k: jnp.concatenate([r16[k, j], rim[k, j]], axis=0)

    send_face(DOWN, read(0), zb, STEPS - 1)
    send_face(UP, read(3), za, STEPS - 1)


class Split:
    def __init__(self, own, rim):
        self.own, self.rim = own, rim

    def whole(self, k, j):
        return jnp.concatenate([self.own[k, j], self.rim[k, j]], axis=0)

    def block(self, k, j, r, cols):
        if r < 16:
            return self.own[k, j, r:r + 8, cols]
        return self.rim[k, j, :, cols]


class Layers:
    def __init__(self, edge, rest):
        self.edge, self.rest = edge, rest

    def whole(self, k, j):
        return self.edge[k] if j == 0 else self.rest[k, j - 1]

    def block(self, k, j, r, cols):
        if j == 0:
            return self.edge[k, r:r + 8, cols]
        return self.rest[k, j - 1, r:r + 8, cols]


class Whole:
    def __init__(self, array):
        self.array = array

    def block(self, k, j, r, cols):
        return self.array[k, j, r:r + 8, cols]


def step_layer(j, state, ads, cap, solid, message, edge, push, moved, store):
    through = []
    for k in range(FIELDS):
        source = j - ALL[k][0]
        if source == -1:
            receive_face(k, DOWN, message, edge, moved.at[k])
        elif source == 4:
            receive_face(k, UP, message, edge, moved.at[k])
        elif ALL[k][1:] == (0, 0):
            through.append(k)
        else:
            moved[k] = shifted(k, state.whole(k, source))
    for r in range(0, ROWS, 8):
        for c in range(0, 256, 128):
            cols = slice(c, c + 128)
            f = [
                state.block(k, j - ALL[k][0], r, cols) if k in through
                else moved[k, r:r + 8, cols]
                for k in range(FIELDS)
            ]
            out, bound = collide(
                f,
                [ads.block(s, j, r, cols) for s in range(2)],
                cap[j, r:r + 8, cols],
                solid[j, r:r + 8, cols] == 0.0,
                push,
            )
            store(r, cols, out, bound)


def edge_kernel(first, edge, *refs):
    (s0, s1), refs = refs[:2], refs[2:]
    state = (Split if first else Layers)(s0, s1)
    ads, refs = (Whole(refs[0]), refs[1:]) if first else (Layers(*refs[:2]), refs[2:])
    cap, solid, zb, r_out, ads_out, zb_out, moved = refs
    push = jnp.where(parity("ax") == 0, 1.0, -1.0)

    def store(r, cols, out, bound):
        for k in range(FIELDS):
            r_out[k, r:r + 8, cols] = out[k]
        for s in range(2):
            ads_out[s, r:r + 8, cols] = bound[s]

    step_layer(0, state, ads, cap, solid, zb, edge, push, moved, store)
    send_face(DOWN, lambda k: r_out[k], zb_out, edge - 1)


def rest_kernel(first, edge, *refs):
    (s0, s1), refs = refs[:2], refs[2:]
    state = (Split if first else Layers)(s0, s1)
    ads, refs = (Whole(refs[0]), refs[1:]) if first else (Layers(*refs[:2]), refs[2:])
    cap, solid, za, r_out, ads_out, za_out, moved = refs
    push = jnp.where(parity("ax") == 0, 1.0, -1.0)
    for j in range(1, 4):
        def store(r, cols, out, bound):
            for k in range(FIELDS):
                r_out[k, j - 1, r:r + 8, cols] = out[k]
            for s in range(2):
                ads_out[s, j - 1, r:r + 8, cols] = bound[s]

        step_layer(j, state, ads, cap, solid, za, edge, push, moved.at[j - 1], store)
    send_face(UP, lambda k: r_out[k, 2], za_out, edge - 1)


def place(p, k, z, pop, sol):
    if k < 19:
        return pop.at[turned(p, k), z]
    s = (k - 19) // 7
    return sol.at[s, turned(p, k) - 19 - 7 * s, z]


def inner_kernel(r_edge, r_rest, ads_edge, ads_rest, pop, sol, ads, stage, sems, ads_sems):
    p = parity("ax")
    state = Layers(r_edge, r_rest)
    copies = []
    for s in range(2):
        for j in range(4):
            source = ads_edge.at[s, 0:16] if j == 0 else ads_rest.at[s, j - 1, 0:16]
            copies.append(
                pltpu.make_async_copy(source, ads.at[s, layer(p, j)], ads_sems.at[s, j])
            )
            copies[-1].start()
    for j in range(4):
        for k in range(FIELDS):
            source = j - ALL[k][0]
            if 0 <= source < 4:
                stage[k, j] = shifted(k, state.whole(k, source))[0:16]
                copies.append(
                    pltpu.make_async_copy(
                        stage.at[k, j], place(p, k, layer(p, j), pop, sol), sems.at[k, j]
                    )
                )
                copies[-1].start()
    for copy in copies:
        copy.wait()


def outer_kernel(pop_in, sol_in, za, zb, pop, sol, sems):
    p = parity("ax")
    copies = []
    for fields, other, message, j in ((UP, DOWN, zb, 0), (DOWN, UP, za, 3)):
        for k in fields:
            i = other.index(MIRROR[k])
            copies.append(
                pltpu.make_async_copy(
                    message.at[16 * i:16 * i + 16],
                    place(p, k, layer(p, j), pop, sol),
                    sems.at[k],
                )
            )
            copies[-1].start()
    for copy in copies:
        copy.wait()


def call(kernel, outs, args, specs=None, out_specs=None, scratch=(), cost=0, aliases=None):
    return pl.pallas_call(
        kernel,
        out_shape=[jax.ShapeDtypeStruct(s, jnp.float32) for s in outs],
        in_specs=specs or [VMEM] * len(args),
        out_specs=out_specs or [VMEM] * len(outs),
        scratch_shapes=list(scratch),
        input_output_aliases=aliases or {},
        cost_estimate=pl.CostEstimate(
            flops=cost, bytes_accessed=cost // 4, transcendentals=0
        ),
        compiler_params=pltpu.CompilerParams(vmem_limit_bytes=16 << 20),
    )(*args)


def swaps(axis):
    count = lax.axis_size(axis)
    inner = [(i, i ^ 1) for i in range(count)]
    outer = [(i, (i + 1) % count if i % 2 else (i - 1) % count) for i in range(count)]
    return inner, outer


def body(populations, solute, adsorbed, capacity, solid):
    inner_z, outer_z = swaps("ax")
    inner_x, outer_x = swaps("xs")
    own = (4, 16, 256)
    f32 = jnp.float32
    r16, ads16, cap16, solid16, xa, xb = call(
        first_kernel,
        [(FIELDS,) + own, (2,) + own, own, own, (MESSAGE, 256), (MESSAGE, 256)],
        [
            pltpu.with_memory_space_constraint(x, pltpu.HBM)
            for x in (populations, solute, adsorbed, capacity, solid)
        ],
        specs=[HBM] * 5,
        scratch=[
            pltpu.VMEM((19,) + own, f32),
            pltpu.VMEM((2, 7) + own, f32),
            pltpu.VMEM((2,) + own, f32),
            pltpu.VMEM(own, f32),
            pltpu.VMEM(own, jnp.int32),
            pltpu.SemaphoreType.DMA((4, 5)),
        ],
    )
    xb = lax.ppermute(xb, "xs", outer_x)
    xa = lax.ppermute(xa, "xs", inner_x)
    tall = (4, ROWS, 256)
    rim, ads24, cap, solid, za, zb = call(
        rim_kernel,
        [(FIELDS, 4, 8, 256), (2,) + tall, tall, tall] + [(face_rows(STEPS - 1), 256)] * 2,
        [r16, ads16, cap16, solid16, xa, xb],
    )
    state, ads = [r16, rim], [ads24]
    for step in range(1, STEPS):
        zb = lax.ppermute(zb, "ax", outer_z)
        za = lax.ppermute(za, "ax", inner_z)
        edge = STEPS - step
        face = (face_rows(edge - 1), 256)
        r_edge, ads_edge, zb = call(
            functools.partial(edge_kernel, step == 1, edge),
            [(FIELDS, ROWS, 256), (2, ROWS, 256), face],
            state + ads + [cap, solid, zb],
            scratch=[pltpu.VMEM((FIELDS, ROWS, 256), f32)],
            cost=1 << 20,
        )
        r_rest, ads_rest, za = call(
            functools.partial(rest_kernel, step == 1, edge),
            [(FIELDS, 3, ROWS, 256), (2, 3, ROWS, 256), face],
            state + ads + [cap, solid, za],
            scratch=[pltpu.VMEM((3, FIELDS, ROWS, 256), f32)],
            cost=3 << 20,
        )
        state, ads = [r_edge, r_rest], [ads_edge, ads_rest]
    zb = lax.ppermute(zb, "ax", outer_z)
    za = lax.ppermute(za, "ax", inner_z)
    pops, species, bound = call(
        inner_kernel,
        [(19,) + own, (2, 7) + own, (2,) + own],
        state + ads,
        out_specs=[ANY] * 3,
        scratch=[
            pltpu.VMEM((FIELDS,) + own, f32),
            pltpu.SemaphoreType.DMA((FIELDS, 4)),
            pltpu.SemaphoreType.DMA((2, 4)),
        ],
        cost=3 << 20,
    )
    pops, species = call(
        outer_kernel,
        [(19,) + own, (2, 7) + own],
        [pops, species, za, zb],
        specs=[ANY, ANY, VMEM, VMEM],
        out_specs=[ANY] * 2,
        scratch=[pltpu.SemaphoreType.DMA((FIELDS,))],
        aliases={0: 0, 1: 1},
    )
    return pops, species, bound


def solution(mesh):
    placed = (
        P(None, "ax", "xs", None),
        P(None, None, "ax", "xs", None),
        P(None, "ax", "xs", None),
        P("ax", "xs", None),
        P("ax", "xs", None),
    )
    return jax.shard_map(
        body,
        mesh=mesh,
        in_specs=placed,
        out_specs=(
            P(None, "ax", "xs", None),
            P(None, None, "ax", "xs", None),
            P(None, "ax", "xs", None),
        ),
        check_vma=False,
    )
```

```python
import functools
import jax
import jax.numpy as jnp
import numpy as np
from jax import lax
from jax.experimental import pallas as pl
from jax.experimental.pallas import tpu as pltpu
from jax.sharding import PartitionSpec as P


STEPS = 4
DEPTH = 4
ROWS = 24
VELOCITY = np.array(
    [
        [0, 0, 0],
        [1, 0, 0],
        [-1, 0, 0],
        [0, 1, 0],
        [0, -1, 0],
        [0, 0, 1],
        [0, 0, -1],
        [1, 1, 0],
        [-1, -1, 0],
        [1, -1, 0],
        [-1, 1, 0],
        [1, 0, 1],
        [-1, 0, -1],
        [1, 0, -1],
        [-1, 0, 1],
        [0, 1, 1],
        [0, -1, -1],
        [0, 1, -1],
        [0, -1, 1],
    ]
)
ALL = [tuple(int(c) for c in v) for v in np.concatenate([VELOCITY, VELOCITY[:7], VELOCITY[:7]])]
FIELDS = len(ALL)
UP = [k for k in range(FIELDS) if ALL[k][0] == 1]
DOWN = [k for k in range(FIELDS) if ALL[k][0] == -1]
OMEGA_SOLUTE = (1.0, 0.7)
ON_RATE = (0.5, 0.2)
OFF_RATE = (0.05, 0.1)
VMEM = pl.BlockSpec(memory_space=pltpu.VMEM)
ANY = pl.BlockSpec(memory_space=pl.ANY)
HBM = pl.BlockSpec(memory_space=pltpu.HBM)
MIRROR = [
    19 * (k >= 19) + 7 * (k >= 26)
    + ALL[: 19 if k < 19 else 7].index((-ALL[k][0],) + ALL[k][1:])
    for k in range(FIELDS)
]


def rim_rows(k, side):
    return DEPTH - 1 + side * ALL[k][1]


def message_plan(side, part):
    pieces = []
    for j in range(4):
        for k in range(FIELDS):
            cz = ALL[k][0]
            if part == 0:
                wanted = not 0 <= j - cz < 4
            else:
                wanted = 0 <= j + cz < 4 and (j + cz == 0) == (part == 1)
            if wanted:
                pieces.append(("r", k, j, rim_rows(k, side)))
        if part == (1 if j == 0 else 2):
            pieces += [(n, i, j, 3) for n, i in (("ads", 0), ("ads", 1), ("cap", 0), ("solid", 0))]
    plan, offset = [], 0
    if part == 2:
        offset = message_shape(1)[0]
    for name, k, j, n in pieces:
        plan.append((name, k, j, n, offset))
        offset += n
    return plan, -(-offset // 8) * 8


def message_shape(part):
    return (message_plan(1, part)[1], 256)


def collide(f, adsorbed, capacity, fluid, push):
    out = [None] * FIELDS
    s = {k: f[k] + f[k + 1] for k in range(1, 19, 2)}
    d = {k: f[k] - f[k + 1] for k in range(1, 19, 2)}
    axis = s[1] + s[3] + s[5]
    edge = (s[7] + s[9]) + (s[11] + s[13]) + (s[15] + s[17])
    density = f[0] + axis + edge
    mz = d[1] + d[7] + d[9] + d[11] + d[13]
    mx = d[3] + d[7] - d[9] + d[15] + d[17]
    my = d[5] + d[11] - d[13] + d[15] - d[17]
    inverse = 1.0 / density
    uz, ux, uy = mz * inverse, mx * inverse, my * inverse
    base = 1.0 - 1.5 * (uz * uz + ux * ux + uy * uy)
    even = (1.25 / 36.0) * density
    rest_even = even * base
    square = 4.5 * even
    oz = (2.25 / 36.0) * mz + (push * (0.003 / 36.0)) * density
    ox = (2.25 / 36.0) * mx
    oy = (2.25 / 36.0) * my
    out[0] = jnp.where(fluid, 12.0 * rest_even - 0.25 * f[0], f[0])
    pairs = {
        1: (uz, oz), 3: (ux, ox), 5: (uy, oy),
        7: (uz + ux, oz + ox), 9: (uz - ux, oz - ox),
        11: (uz + uy, oz + oy), 13: (uz - uy, oz - oy),
        15: (ux + uy, ox + oy), 17: (ux - uy, ox - oy),
    }
    for k, (u, o) in pairs.items():
        e = rest_even + square * (u * u)
        if k < 7:
            e, o = e + e, o + o
        a = e - 0.125 * s[k]
        b = o + 0.125 * d[k]
        out[k] = jnp.where(fluid, a + b, f[k + 1])
        out[k + 1] = jnp.where(fluid, a - b, f[k])
    occupied = adsorbed[0] + adsorbed[1]
    free = capacity - occupied
    bound = []
    for kind in range(2):
        g = f[19 + 7 * kind: 26 + 7 * kind]
        total = g[0] + (g[1] + g[2]) + (g[3] + g[4]) + (g[5] + g[6])
        uptake = ON_RATE[kind] * total * free - OFF_RATE[kind] * adsorbed[kind]
        bound.append(jnp.where(fluid, adsorbed[kind] + uptake, adsorbed[kind]))
        omega = OMEGA_SOLUTE[kind]
        moved = total if omega == 1.0 else omega * total
        share = 0.125 * (moved - uptake)
        drift = 0.5 * moved

        def kept(h):
            return 0.0 if omega == 1.0 else (1.0 - omega) * h

        out[19 + 7 * kind] = jnp.where(fluid, kept(g[0]) + (share + share), g[0])
        for j, u in ((1, uz), (3, ux), (5, uy)):
            o = drift * u
            out[19 + 7 * kind + j] = jnp.where(fluid, kept(g[j]) + (share + o), g[j + 1])
            out[19 + 7 * kind + j + 1] = jnp.where(fluid, kept(g[j + 1]) + (share - o), g[j])
    return out, bound


def parity(axis):
    return lax.rem(lax.axis_index(axis), 2)


def turned(p, k):
    return jnp.where(p == 0, k, MIRROR[k]) if MIRROR[k] != k else k


def layer(p, j):
    return jnp.where(p == 0, j, 3 - j)


def first_kernel(
    pop, sol, ads, cap, solid, r_out, ads_out, cap_out, solid_out, za, zb, *messages
):
    pop_in, sol_in, ads_in, cap_in, solid_in, sems = messages[-6:]
    p = parity("ax")
    push = jnp.where(p == 0, 1.0, -1.0)
    copies = []
    for j in range(4):
        z = layer(p, j)
        pairs = [
            (pop.at[:, z], pop_in.at[:, j]),
            (sol.at[:, :, z], sol_in.at[:, :, j]),
            (ads.at[:, z], ads_in.at[:, j]),
            (cap.at[z], cap_in.at[j]),
            (solid.at[z], solid_in.at[j]),
        ]
        copies.append([
            pltpu.make_async_copy(a, b, sems.at[j, i]) for i, (a, b) in enumerate(pairs)
        ])
    for group in copies:
        for copy in group:
            copy.start()
    for j in range(4):
        for copy in copies[j]:
            copy.wait()
        for r in range(0, 16, 8):
            for c in range(0, 256, 128):
                at = (j, slice(r, r + 8), slice(c, c + 128))
                f = [pop_in[(turned(p, k),) + at] for k in range(19)]
                f += [
                    sol_in[(s, turned(p, 19 + 7 * s + k) - 19 - 7 * s) + at]
                    for s in range(2) for k in range(7)
                ]
                cap_out[at] = cap_in[at]
                solid_out[at] = solid_in[at].astype(jnp.float32)
                out, bound = collide(
                    f, [ads_in[(0,) + at], ads_in[(1,) + at]], cap_in[at],
                    solid_in[at] == 0, push,
                )
                for k in range(FIELDS):
                    r_out[(k,) + at] = out[k]
                for s in range(2):
                    ads_out[(s,) + at] = bound[s]

    for fields, j, message in ((DOWN, 0, zb), (UP, 3, za)):
        for i, k in enumerate(fields):
            message[16 * i:16 * i + 16, :] = turn_columns(k, r_out[k, j])
    sources = {"r": r_out, "ads": ads_out, "cap": cap_out, "solid": solid_out}
    messages = messages[:-6]
    for part in (1, 2):
        pack(lambda name, at: sources[name][at], part, *messages[:2])
        messages = messages[2:] or messages


def pack(read, part, xa, xb):
    def fill(side, message):
        for name, k, j, n, offset in message_plan(side, part)[0]:
            rows = slice(16 - n, 16) if side == 1 else slice(0, n)
            at = (k, j) if name in ("r", "ads") else (j,)
            message[offset:offset + n, :] = read(name, at + (rows, slice(None)))

    q = parity("xs")

    @pl.when(q == 0)
    def _():
        fill(1, xa)
        fill(-1, xb)

    @pl.when(q == 1)
    def _():
        fill(-1, xa)
        fill(1, xb)


def unpack(part, xa, xb, put):
    def empty(side, message):
        for name, k, j, n, offset in message_plan(side, part)[0]:
            put(name, k, j, 8 - n if side == 1 else 0, message[offset:offset + n, :])

    q = parity("xs")

    @pl.when(q == 0)
    def _():
        empty(-1, xa)
        empty(1, xb)

    @pl.when(q == 1)
    def _():
        empty(1, xa)
        empty(-1, xb)


def turn_rows(k, v):
    return pltpu.roll(v, ALL[k][1] % ROWS, 0) if ALL[k][1] else v


def turn_columns(k, v):
    return pltpu.roll(v, ALL[k][2] % 256, 1) if ALL[k][2] else v


def shifted(k, v):
    return turn_columns(k, turn_rows(k, v))


def face_rows(edge):
    return -(-7 * (16 + 2 * edge) // 8) * 8


def send_face(fields, read, message, edge):
    for i, k in enumerate(fields):
        v = shifted(k, read(k))
        message[16 * i:16 * i + 16, :] = v[0:16]
        if edge:
            at = 112 + 2 * edge * i
            message[at:at + edge, :] = v[16:16 + edge]
            message[at + edge:at + 2 * edge, :] = v[24 - edge:24]


def receive_face(k, message, edge, moved):
    i = place_in_face(k)
    moved[0:16, :] = message[16 * i:16 * i + 16, :]
    if edge:
        at = 112 + 2 * edge * i
        moved[16:16 + edge, :] = message[at:at + edge, :]
        moved[24 - edge:24, :] = message[at + edge:at + 2 * edge, :]


def receive_first_faces(j, message, xa0, xb0, moved):
    def put(name, k, layer, low, piece):
        if layer == j:
            moved[k, 16 + low:16 + low + piece.shape[0], :] = piece

    unpack(0, xa0, xb0, put)
    for k in UP if j == 0 else DOWN:
        i = place_in_face(k)
        if ALL[k][1]:
            rows = jnp.concatenate([message[16 * i:16 * i + 16, :], moved[k, 16:24, :]], axis=0)
            moved[k] = turn_rows(k, rows)
        else:
            moved[k, 0:16, :] = message[16 * i:16 * i + 16, :]


def place_in_face(k):
    return (DOWN if ALL[k][0] == 1 else UP).index(MIRROR[k])


def corner_kernel(za, zb, xa0, xb0):
    def read(name, at):
        i = 16 * place_in_face(at[0])
        return (zb if at[1] == 0 else za)[i + at[2].start:i + at[2].stop, :]

    pack(read, 0, xa0, xb0)


def rim_kernel(part, xa, xb, rim, rim_ads, rim_cap, rim_solid):
    arrays = {"r": rim, "ads": rim_ads, "cap": rim_cap, "solid": rim_solid}

    def put(name, k, j, low, piece):
        at = (k, j) if name in ("r", "ads") else (j,)
        arrays[name][at + (slice(low, low + piece.shape[0]), slice(None))] = piece

    unpack(part, xa, xb, put)


class Split:
    def __init__(self, own, first, second):
        self.own, self.first, self.second = own, first, second

    def rim(self, k, j):
        cz = 0 if k is None or self.own.shape[0] == 2 else ALL[k][0]
        return self.first if j + cz == 0 else self.second

    def whole(self, k, j):
        return jnp.concatenate([self.own[k, j], self.rim(k, j)[k, j]], axis=0)

    def block(self, k, j, r, cols):
        at = (j,) if k is None else (k, j)
        if r < 16:
            return self.own[at + (slice(r, r + 8), cols)]
        return self.rim(k, j)[at + (slice(0, 8), cols)]


class Layers:
    def __init__(self, edge, rest):
        self.edge, self.rest = edge, rest

    def whole(self, k, j):
        return self.edge[k] if j == 0 else self.rest[k, j - 1]

    def block(self, k, j, r, cols):
        if j == 0:
            return self.edge[k, r:r + 8, cols]
        return self.rest[k, j - 1, r:r + 8, cols]


def step_layer(j, state, ads, cap, solid, message, corners, edge, push, moved, store):
    through = []
    if corners and j in (0, 3):
        receive_first_faces(j, message, *corners, moved)
    for k in range(FIELDS):
        source = j - ALL[k][0]
        if source == -1 or source == 4:
            if not corners:
                receive_face(k, message, edge, moved.at[k])
        elif ALL[k][1:] == (0, 0):
            through.append(k)
        else:
            moved[k] = shifted(k, state.whole(k, source))
    for r in range(0, ROWS, 8):
        for c in range(0, 256, 128):
            cols = slice(c, c + 128)
            f = [
                state.block(k, j - ALL[k][0], r, cols) if k in through
                else moved[k, r:r + 8, cols]
                for k in range(FIELDS)
            ]
            out, bound = collide(
                f,
                [ads.block(s, j, r, cols) for s in range(2)],
                cap.block(None, j, r, cols),
                solid.block(None, j, r, cols) == 0.0,
                push,
            )
            store(r, cols, out, bound)


def edge_kernel(first, edge, *refs):
    if first:
        r16, ads16, rim, rim_ads, xa0, xb0 = refs[:6]
        state, ads = Split(r16, rim, None), Split(ads16, rim_ads, None)
        corners = (xa0, xb0)
        refs = refs[6:]
    else:
        state, ads, corners = Layers(*refs[:2]), Layers(*refs[2:4]), ()
        refs = refs[4:]
    cap16, solid16, rim_cap, rim_solid, zb, r_out, ads_out, zb_out, moved = refs
    cap, solid = Split(cap16, rim_cap, None), Split(solid16, rim_solid, None)
    push = jnp.where(parity("ax") == 0, 1.0, -1.0)

    def store(r, cols, out, bound):
        for k in range(FIELDS):
            r_out[k, r:r + 8, cols] = out[k]
        for s in range(2):
            ads_out[s, r:r + 8, cols] = bound[s]

    step_layer(0, state, ads, cap, solid, zb, corners, edge, push, moved, store)
    send_face(DOWN, lambda k: r_out[k], zb_out, edge - 1)


def rest_kernel(first, edge, *refs):
    refs = list(refs)
    if first:
        edge_ref, r16, ads16, low, low_ads, xa0, xb0, high, high_ads = refs[:9]
        state, ads = Split(r16, low, high), Split(ads16, low_ads, high_ads)
        corners = (xa0, xb0)
        refs = refs[9:]
    else:
        state, ads, corners = Layers(*refs[:2]), Layers(*refs[2:4]), ()
        refs = refs[4:]
    cap16, solid16, low_cap, low_solid, high_cap, high_solid = refs[:6]
    cap, solid = Split(cap16, low_cap, high_cap), Split(solid16, low_solid, high_solid)
    za, r_out, ads_out, za_out, moved = refs[6:]
    push = jnp.where(parity("ax") == 0, 1.0, -1.0)
    for j in range(1, 4):
        def store(r, cols, out, bound):
            for k in range(FIELDS):
                r_out[k, j - 1, r:r + 8, cols] = out[k]
            for s in range(2):
                ads_out[s, j - 1, r:r + 8, cols] = bound[s]

        step_layer(j, state, ads, cap, solid, za, corners, edge, push, moved.at[j - 1], store)
    send_face(UP, lambda k: r_out[k, 2], za_out, edge - 1)


def place(p, k, z, pop, sol):
    if k < 19:
        return pop.at[turned(p, k), z]
    s = (k - 19) // 7
    return sol.at[s, turned(p, k) - 19 - 7 * s, z]


def inner_kernel(r_edge, r_rest, ads_edge, ads_rest, pop, sol, ads, stage, sems, ads_sems):
    p = parity("ax")
    state = Layers(r_edge, r_rest)
    copies = []
    for s in range(2):
        for j in range(4):
            source = ads_edge.at[s, 0:16] if j == 0 else ads_rest.at[s, j - 1, 0:16]
            copies.append(
                pltpu.make_async_copy(source, ads.at[s, layer(p, j)], ads_sems.at[s, j])
            )
            copies[-1].start()
    for j in range(4):
        for k in range(FIELDS):
            source = j - ALL[k][0]
            if 0 <= source < 4:
                stage[k, j] = shifted(k, state.whole(k, source))[0:16]
                copies.append(
                    pltpu.make_async_copy(
                        stage.at[k, j], place(p, k, layer(p, j), pop, sol), sems.at[k, j]
                    )
                )
                copies[-1].start()
    for copy in copies:
        copy.wait()


def outer_kernel(pop_in, sol_in, za, zb, pop, sol, sems):
    p = parity("ax")
    copies = []
    for fields, message, j in ((UP, zb, 0), (DOWN, za, 3)):
        for k in fields:
            i = place_in_face(k)
            copies.append(
                pltpu.make_async_copy(
                    message.at[16 * i:16 * i + 16],
                    place(p, k, layer(p, j), pop, sol),
                    sems.at[k],
                )
            )
            copies[-1].start()
    for copy in copies:
        copy.wait()


def call(kernel, outs, args, specs=None, out_specs=None, scratch=(), cost=0, aliases=None):
    return pl.pallas_call(
        kernel,
        out_shape=[jax.ShapeDtypeStruct(s, jnp.float32) for s in outs],
        in_specs=specs or [VMEM] * len(args),
        out_specs=out_specs or [VMEM] * len(outs),
        scratch_shapes=list(scratch),
        input_output_aliases=aliases or {},
        cost_estimate=pl.CostEstimate(
            flops=cost, bytes_accessed=cost // 4, transcendentals=0
        ),
        compiler_params=pltpu.CompilerParams(vmem_limit_bytes=16 << 20),
    )(*args)


def swaps(axis):
    count = lax.axis_size(axis)
    inner = [(i, i ^ 1) for i in range(count)]
    outer = [(i, (i + 1) % count if i % 2 else (i - 1) % count) for i in range(count)]
    return inner, outer


def body(populations, solute, adsorbed, capacity, solid):
    inner_z, outer_z = swaps("ax")
    inner_x, outer_x = swaps("xs")
    own = (4, 16, 256)
    f32 = jnp.float32
    bulk = [message_shape(2)] * 2
    r16, ads16, cap16, solid16, za, zb, *messages = call(
        first_kernel,
        [(FIELDS,) + own, (2,) + own, own, own] + [(112, 256)] * 2 + bulk,
        [
            pltpu.with_memory_space_constraint(x, pltpu.HBM)
            for x in (populations, solute, adsorbed, capacity, solid)
        ],
        specs=[HBM] * 5,
        scratch=[
            pltpu.VMEM((19,) + own, f32),
            pltpu.VMEM((2, 7) + own, f32),
            pltpu.VMEM((2,) + own, f32),
            pltpu.VMEM(own, f32),
            pltpu.VMEM(own, jnp.int32),
            pltpu.SemaphoreType.DMA((4, 5)),
        ],
    )
    zb = lax.ppermute(zb, "ax", outer_z)
    za = lax.ppermute(za, "ax", inner_z)
    messages = [
        lax.ppermute(m, "xs", (inner_x, outer_x)[i % 2]) for i, m in enumerate(messages)
    ]
    xa0, xb0 = call(corner_kernel, [message_shape(0)] * 2, [za, zb], cost=1 << 36)
    xb0 = lax.ppermute(xb0, "xs", outer_x)
    xa0 = lax.ppermute(xa0, "xs", inner_x)
    rims = [(FIELDS, 4, 8, 256), (2, 4, 8, 256), (4, 8, 256), (4, 8, 256)]
    low, low_ads, low_cap, low_solid = call(
        functools.partial(rim_kernel, 1), rims, messages[:2], cost=1 << 18
    )
    high, high_ads, high_cap, high_solid = call(
        functools.partial(rim_kernel, 2), rims, messages[-2:], cost=1 << 18
    )
    sites = [cap16, solid16, low_cap, low_solid]
    more = [high_cap, high_solid]
    for step in range(1, STEPS):
        first = step == 1
        if first:
            edge_args = [r16, ads16, low, low_ads, xa0, xb0]
            rest_args = edge_args + [high, high_ads]
        else:
            zb = lax.ppermute(zb, "ax", outer_z)
            za = lax.ppermute(za, "ax", inner_z)
            edge_args = rest_args = [r_edge, r_rest, ads_edge, ads_rest]
        edge = STEPS - step
        face = (face_rows(edge - 1), 256)
        r_edge, ads_edge, zb = call(
            functools.partial(edge_kernel, first, edge),
            [(FIELDS, ROWS, 256), (2, ROWS, 256), face],
            edge_args + sites + [zb],
            scratch=[pltpu.VMEM((FIELDS, ROWS, 256), f32)],
            cost=1 << 20,
        )
        r_rest, ads_rest, za = call(
            functools.partial(rest_kernel, first, edge),
            [(FIELDS, 3, ROWS, 256), (2, 3, ROWS, 256), face],
            [r_edge] * first + rest_args + sites + more + [za],
            scratch=[pltpu.VMEM((3, FIELDS, ROWS, 256), f32)],
            cost=3 << 20,
        )
    zb = lax.ppermute(zb, "ax", outer_z)
    za = lax.ppermute(za, "ax", inner_z)
    pops, species, bound = call(
        inner_kernel,
        [(19,) + own, (2, 7) + own, (2,) + own],
        [r_edge, r_rest, ads_edge, ads_rest],
        out_specs=[ANY] * 3,
        scratch=[
            pltpu.VMEM((FIELDS,) + own, f32),
            pltpu.SemaphoreType.DMA((FIELDS, 4)),
            pltpu.SemaphoreType.DMA((2, 4)),
        ],
        cost=3 << 20,
    )
    pops, species = call(
        outer_kernel,
        [(19,) + own, (2, 7) + own],
        [pops, species, za, zb],
        specs=[ANY, ANY, VMEM, VMEM],
        out_specs=[ANY] * 2,
        scratch=[pltpu.SemaphoreType.DMA((FIELDS,))],
        aliases={0: 0, 1: 1},
    )
    return pops, species, bound


def solution(mesh):
    placed = (
        P(None, "ax", "xs", None),
        P(None, None, "ax", "xs", None),
        P(None, "ax", "xs", None),
        P("ax", "xs", None),
        P("ax", "xs", None),
    )
    return jax.shard_map(
        body,
        mesh=mesh,
        in_specs=placed,
        out_specs=(
            P(None, "ax", "xs", None),
            P(None, None, "ax", "xs", None),
            P(None, "ax", "xs", None),
        ),
        check_vma=False,
    )
```

```python
import functools
import jax
import jax.numpy as jnp
import numpy as np
from jax import lax
from jax.experimental import pallas as pl
from jax.experimental.pallas import tpu as pltpu
from jax.sharding import PartitionSpec as P


STEPS = 4
DEPTH = 4
ROWS = 24
VELOCITY = np.array(
    [
        [0, 0, 0],
        [1, 0, 0],
        [-1, 0, 0],
        [0, 1, 0],
        [0, -1, 0],
        [0, 0, 1],
        [0, 0, -1],
        [1, 1, 0],
        [-1, -1, 0],
        [1, -1, 0],
        [-1, 1, 0],
        [1, 0, 1],
        [-1, 0, -1],
        [1, 0, -1],
        [-1, 0, 1],
        [0, 1, 1],
        [0, -1, -1],
        [0, 1, -1],
        [0, -1, 1],
    ]
)
ALL = [tuple(int(c) for c in v) for v in np.concatenate([VELOCITY, VELOCITY[:7], VELOCITY[:7]])]
FIELDS = len(ALL)
UP = [k for k in range(FIELDS) if ALL[k][0] == 1]
DOWN = [k for k in range(FIELDS) if ALL[k][0] == -1]
OMEGA_SOLUTE = (1.0, 0.7)
ON_RATE = (0.5, 0.2)
OFF_RATE = (0.05, 0.1)
VMEM = pl.BlockSpec(memory_space=pltpu.VMEM)
ANY = pl.BlockSpec(memory_space=pl.ANY)
HBM = pl.BlockSpec(memory_space=pltpu.HBM)
MIRROR = [
    19 * (k >= 19) + 7 * (k >= 26)
    + ALL[: 19 if k < 19 else 7].index((-ALL[k][0],) + ALL[k][1:])
    for k in range(FIELDS)
]


def rim_rows(k, side):
    return DEPTH - 1 + side * ALL[k][1]


def message_plan(side, part):
    pieces = []
    for j in range(4):
        for k in range(FIELDS):
            cz = ALL[k][0]
            if part == 0:
                wanted = not 0 <= j - cz < 4
            else:
                wanted = 0 <= j + cz < 4 and (j + cz == 0) == (part == 1)
            if wanted:
                pieces.append(("r", k, j, rim_rows(k, side)))
        if part == (1 if j == 0 else 2):
            pieces += [(n, i, j, 3) for n, i in (("ads", 0), ("ads", 1), ("cap", 0), ("solid", 0))]
    plan, offset = [], 0
    if part == 2:
        offset = message_shape(1)[0]
    for name, k, j, n in pieces:
        plan.append((name, k, j, n, offset))
        offset += n
    return plan, -(-offset // 8) * 8


def message_shape(part):
    return (message_plan(1, part)[1], 256)


def collide(f, adsorbed, capacity, fluid, push):
    out = [None] * FIELDS
    s = {k: f[k] + f[k + 1] for k in range(1, 19, 2)}
    d = {k: f[k] - f[k + 1] for k in range(1, 19, 2)}
    axis = s[1] + s[3] + s[5]
    edge = (s[7] + s[9]) + (s[11] + s[13]) + (s[15] + s[17])
    density = f[0] + axis + edge
    mz = d[1] + d[7] + d[9] + d[11] + d[13]
    mx = d[3] + d[7] - d[9] + d[15] + d[17]
    my = d[5] + d[11] - d[13] + d[15] - d[17]
    inverse = 1.0 / density
    uz, ux, uy = mz * inverse, mx * inverse, my * inverse
    base = 1.0 - 1.5 * (uz * uz + ux * ux + uy * uy)
    even = (1.25 / 36.0) * density
    rest_even = even * base
    square = 4.5 * even
    oz = (2.25 / 36.0) * mz + (push * (0.003 / 36.0)) * density
    ox = (2.25 / 36.0) * mx
    oy = (2.25 / 36.0) * my
    out[0] = jnp.where(fluid, 12.0 * rest_even - 0.25 * f[0], f[0])
    pairs = {
        1: (uz, oz), 3: (ux, ox), 5: (uy, oy),
        7: (uz + ux, oz + ox), 9: (uz - ux, oz - ox),
        11: (uz + uy, oz + oy), 13: (uz - uy, oz - oy),
        15: (ux + uy, ox + oy), 17: (ux - uy, ox - oy),
    }
    for k, (u, o) in pairs.items():
        e = rest_even + square * (u * u)
        if k < 7:
            e, o = e + e, o + o
        a = e - 0.125 * s[k]
        b = o + 0.125 * d[k]
        out[k] = jnp.where(fluid, a + b, f[k + 1])
        out[k + 1] = jnp.where(fluid, a - b, f[k])
    occupied = adsorbed[0] + adsorbed[1]
    free = capacity - occupied
    bound = []
    for kind in range(2):
        g = f[19 + 7 * kind: 26 + 7 * kind]
        total = g[0] + (g[1] + g[2]) + (g[3] + g[4]) + (g[5] + g[6])
        uptake = ON_RATE[kind] * total * free - OFF_RATE[kind] * adsorbed[kind]
        bound.append(jnp.where(fluid, adsorbed[kind] + uptake, adsorbed[kind]))
        omega = OMEGA_SOLUTE[kind]
        moved = total if omega == 1.0 else omega * total
        share = 0.125 * (moved - uptake)
        drift = 0.5 * moved

        def kept(h):
            return 0.0 if omega == 1.0 else (1.0 - omega) * h

        out[19 + 7 * kind] = jnp.where(fluid, kept(g[0]) + (share + share), g[0])
        for j, u in ((1, uz), (3, ux), (5, uy)):
            o = drift * u
            out[19 + 7 * kind + j] = jnp.where(fluid, kept(g[j]) + (share + o), g[j + 1])
            out[19 + 7 * kind + j + 1] = jnp.where(fluid, kept(g[j + 1]) + (share - o), g[j])
    return out, bound


def parity(axis):
    return lax.rem(lax.axis_index(axis), 2)


def turned(p, k):
    return jnp.where(p == 0, k, MIRROR[k]) if MIRROR[k] != k else k


def layer(p, j):
    return jnp.where(p == 0, j, 3 - j)


def first_kernel(
    pop, sol, ads, cap, solid, r_out, ads_out, cap_out, solid_out, za, zb,
    xb, xa, pop_in, sol_in, ads_in, cap_in, solid_in, sems,
):
    sources = {"r": r_out, "ads": ads_out, "cap": cap_out, "solid": solid_out}
    p = parity("ax")
    push = jnp.where(p == 0, 1.0, -1.0)
    copies = []
    for j in range(4):
        z = layer(p, j)
        pairs = [
            (pop.at[:, z], pop_in.at[:, j]),
            (sol.at[:, :, z], sol_in.at[:, :, j]),
            (ads.at[:, z], ads_in.at[:, j]),
            (cap.at[z], cap_in.at[j]),
            (solid.at[z], solid_in.at[j]),
        ]
        copies.append([
            pltpu.make_async_copy(a, b, sems.at[j, i]) for i, (a, b) in enumerate(pairs)
        ])
    for group in copies:
        for copy in group:
            copy.start()
    for j in range(4):
        for copy in copies[j]:
            copy.wait()
        for r in range(0, 16, 8):
            for c in range(0, 256, 128):
                at = (j, slice(r, r + 8), slice(c, c + 128))
                f = [pop_in[(turned(p, k),) + at] for k in range(19)]
                f += [
                    sol_in[(s, turned(p, 19 + 7 * s + k) - 19 - 7 * s) + at]
                    for s in range(2) for k in range(7)
                ]
                cap_out[at] = cap_in[at]
                solid_out[at] = solid_in[at].astype(jnp.float32)
                out, bound = collide(
                    f, [ads_in[(0,) + at], ads_in[(1,) + at]], cap_in[at],
                    solid_in[at] == 0, push,
                )
                for k in range(FIELDS):
                    r_out[(k,) + at] = out[k]
                for s in range(2):
                    ads_out[(s,) + at] = bound[s]

        if j == 0 or j == 3:
            fields, message = (DOWN, zb) if j == 0 else (UP, za)
            for i, k in enumerate(fields):
                message[16 * i:16 * i + 16, :] = turn_columns(k, r_out[k, j])
        for part in (1, 2):
            pack(lambda name, at: sources[name][at], part, xa, xb, (j,))


def pack(read, part, xa, xb, layers=range(4)):
    def fill(side, message):
        for name, k, j, n, offset in message_plan(side, part)[0]:
            if j not in layers:
                continue
            rows = slice(16 - n, 16) if side == 1 else slice(0, n)
            at = (k, j) if name in ("r", "ads") else (j,)
            message[offset:offset + n, :] = read(name, at + (rows, slice(None)))

    q = parity("xs")

    @pl.when(q == 0)
    def _():
        fill(1, xa)
        fill(-1, xb)

    @pl.when(q == 1)
    def _():
        fill(-1, xa)
        fill(1, xb)


def unpack(part, xa, xb, put):
    def empty(side, message):
        for name, k, j, n, offset in message_plan(side, part)[0]:
            put(name, k, j, 8 - n if side == 1 else 0, message[offset:offset + n, :])

    q = parity("xs")

    @pl.when(q == 0)
    def _():
        empty(-1, xa)
        empty(1, xb)

    @pl.when(q == 1)
    def _():
        empty(1, xa)
        empty(-1, xb)


def turn_rows(k, v):
    return pltpu.roll(v, ALL[k][1] % ROWS, 0) if ALL[k][1] else v


def turn_columns(k, v):
    return pltpu.roll(v, ALL[k][2] % 256, 1) if ALL[k][2] else v


def shifted(k, v):
    return turn_columns(k, turn_rows(k, v))


def face_rows(edge):
    return -(-7 * (16 + 2 * edge) // 8) * 8


def send_face(fields, read, message, edge):
    for i, k in enumerate(fields):
        v = shifted(k, read(k))
        message[16 * i:16 * i + 16, :] = v[0:16]
        if edge:
            at = 112 + 2 * edge * i
            message[at:at + edge, :] = v[16:16 + edge]
            message[at + edge:at + 2 * edge, :] = v[24 - edge:24]


def receive_face(k, message, edge, moved):
    i = place_in_face(k)
    moved[0:16, :] = message[16 * i:16 * i + 16, :]
    if edge:
        at = 112 + 2 * edge * i
        moved[16:16 + edge, :] = message[at:at + edge, :]
        moved[24 - edge:24, :] = message[at + edge:at + 2 * edge, :]


def receive_first_faces(j, message, xa0, xb0, moved):
    def put(name, k, layer, low, piece):
        if layer == j:
            moved[k, 16 + low:16 + low + piece.shape[0], :] = piece

    unpack(0, xa0, xb0, put)
    for k in UP if j == 0 else DOWN:
        i = place_in_face(k)
        if ALL[k][1]:
            rows = jnp.concatenate([message[16 * i:16 * i + 16, :], moved[k, 16:24, :]], axis=0)
            moved[k] = turn_rows(k, rows)
        else:
            moved[k, 0:16, :] = message[16 * i:16 * i + 16, :]


def place_in_face(k):
    return (DOWN if ALL[k][0] == 1 else UP).index(MIRROR[k])


def token_kernel(message, token):
    token[...] = message[0:8, 0:128]


def corner_kernel(za, zb, token, xb0, xa0):
    def read(name, at):
        i = 16 * place_in_face(at[0])
        return (zb if at[1] == 0 else za)[i + at[2].start:i + at[2].stop, :]

    pack(read, 0, xa0, xb0)


def rim_kernel(part, xb, xa, rim, rim_ads, rim_cap, rim_solid):
    arrays = {"r": rim, "ads": rim_ads, "cap": rim_cap, "solid": rim_solid}

    def put(name, k, j, low, piece):
        at = (k, j) if name in ("r", "ads") else (j,)
        arrays[name][at + (slice(low, low + piece.shape[0]), slice(None))] = piece

    unpack(part, xa, xb, put)


class Split:
    def __init__(self, own, first, second):
        self.own, self.first, self.second = own, first, second

    def rim(self, k, j):
        cz = 0 if k is None or self.own.shape[0] == 2 else ALL[k][0]
        return self.first if j + cz == 0 else self.second

    def whole(self, k, j):
        return jnp.concatenate([self.own[k, j], self.rim(k, j)[k, j]], axis=0)

    def block(self, k, j, r, cols):
        at = (j,) if k is None else (k, j)
        if r < 16:
            return self.own[at + (slice(r, r + 8), cols)]
        return self.rim(k, j)[at + (slice(0, 8), cols)]


class Layers:
    def __init__(self, edge, rest):
        self.edge, self.rest = edge, rest

    def whole(self, k, j):
        return self.edge[k] if j == 0 else self.rest[k, j - 1]

    def block(self, k, j, r, cols):
        if j == 0:
            return self.edge[k, r:r + 8, cols]
        return self.rest[k, j - 1, r:r + 8, cols]


def step_layer(j, state, ads, cap, solid, message, corners, edge, push, moved, store):
    through = []
    if corners and j in (0, 3):
        receive_first_faces(j, message, *corners, moved)
    for k in range(FIELDS):
        source = j - ALL[k][0]
        if source == -1 or source == 4:
            if not corners:
                receive_face(k, message, edge, moved.at[k])
        elif ALL[k][1:] == (0, 0):
            through.append(k)
        else:
            moved[k] = shifted(k, state.whole(k, source))
    for r in range(0, ROWS, 8):
        for c in range(0, 256, 128):
            cols = slice(c, c + 128)
            f = [
                state.block(k, j - ALL[k][0], r, cols) if k in through
                else moved[k, r:r + 8, cols]
                for k in range(FIELDS)
            ]
            out, bound = collide(
                f,
                [ads.block(s, j, r, cols) for s in range(2)],
                cap.block(None, j, r, cols),
                solid.block(None, j, r, cols) == 0.0,
                push,
            )
            store(r, cols, out, bound)


def edge_kernel(first, edge, *refs):
    if first:
        r16, ads16, rim, rim_ads, xb0, xa0 = refs[:6]
        state, ads = Split(r16, rim, None), Split(ads16, rim_ads, None)
        corners = (xa0, xb0)
        refs = refs[6:]
    else:
        state, ads, corners = Layers(*refs[:2]), Layers(*refs[2:4]), ()
        refs = refs[4:]
    cap16, solid16, rim_cap, rim_solid, zb, r_out, ads_out, zb_out, moved = refs
    cap, solid = Split(cap16, rim_cap, None), Split(solid16, rim_solid, None)
    push = jnp.where(parity("ax") == 0, 1.0, -1.0)

    def store(r, cols, out, bound):
        for k in range(FIELDS):
            r_out[k, r:r + 8, cols] = out[k]
        for s in range(2):
            ads_out[s, r:r + 8, cols] = bound[s]

    step_layer(0, state, ads, cap, solid, zb, corners, edge, push, moved, store)
    send_face(DOWN, lambda k: r_out[k], zb_out, edge - 1)


def rest_kernel(first, edge, *refs):
    refs = list(refs)
    if first:
        edge_ref, r16, ads16, low, low_ads, xb0, xa0, high, high_ads = refs[:9]
        state, ads = Split(r16, low, high), Split(ads16, low_ads, high_ads)
        corners = (xa0, xb0)
        refs = refs[9:]
    else:
        state, ads, corners = Layers(*refs[:2]), Layers(*refs[2:4]), ()
        refs = refs[4:]
    cap16, solid16, low_cap, low_solid, high_cap, high_solid = refs[:6]
    cap, solid = Split(cap16, low_cap, high_cap), Split(solid16, low_solid, high_solid)
    za, r_out, ads_out, za_out, moved = refs[6:]
    push = jnp.where(parity("ax") == 0, 1.0, -1.0)
    for j in range(1, 4):
        def store(r, cols, out, bound):
            for k in range(FIELDS):
                r_out[k, j - 1, r:r + 8, cols] = out[k]
            for s in range(2):
                ads_out[s, j - 1, r:r + 8, cols] = bound[s]

        step_layer(j, state, ads, cap, solid, za, corners, edge, push, moved.at[j - 1], store)
    send_face(UP, lambda k: r_out[k, 2], za_out, edge - 1)


def place(p, k, z, pop, sol):
    if k < 19:
        return pop.at[turned(p, k), z]
    s = (k - 19) // 7
    return sol.at[s, turned(p, k) - 19 - 7 * s, z]


def inner_kernel(r_edge, r_rest, ads_edge, ads_rest, pop, sol, ads, stage, sems, ads_sems):
    p = parity("ax")
    state = Layers(r_edge, r_rest)
    copies = []
    for s in range(2):
        for j in range(4):
            source = ads_edge.at[s, 0:16] if j == 0 else ads_rest.at[s, j - 1, 0:16]
            copies.append(
                pltpu.make_async_copy(source, ads.at[s, layer(p, j)], ads_sems.at[s, j])
            )
            copies[-1].start()
    for j in range(4):
        for k in range(FIELDS):
            source = j - ALL[k][0]
            if 0 <= source < 4:
                stage[k, j] = shifted(k, state.whole(k, source))[0:16]
                copies.append(
                    pltpu.make_async_copy(
                        stage.at[k, j], place(p, k, layer(p, j), pop, sol), sems.at[k, j]
                    )
                )
                copies[-1].start()
    for copy in copies:
        copy.wait()


def outer_kernel(pop_in, sol_in, za, zb, pop, sol, sems):
    p = parity("ax")
    copies = []
    for fields, message, j in ((UP, zb, 0), (DOWN, za, 3)):
        for k in fields:
            i = place_in_face(k)
            copies.append(
                pltpu.make_async_copy(
                    message.at[16 * i:16 * i + 16],
                    place(p, k, layer(p, j), pop, sol),
                    sems.at[k],
                )
            )
            copies[-1].start()
    for copy in copies:
        copy.wait()


def call(kernel, outs, args, specs=None, out_specs=None, scratch=(), cost=0, aliases=None):
    return pl.pallas_call(
        kernel,
        out_shape=[jax.ShapeDtypeStruct(s, jnp.float32) for s in outs],
        in_specs=specs or [VMEM] * len(args),
        out_specs=out_specs or [VMEM] * len(outs),
        scratch_shapes=list(scratch),
        input_output_aliases=aliases or {},
        cost_estimate=pl.CostEstimate(
            flops=cost, bytes_accessed=cost // 4, transcendentals=0
        ),
        compiler_params=pltpu.CompilerParams(vmem_limit_bytes=16 << 20),
    )(*args)


def swaps(axis):
    count = lax.axis_size(axis)
    inner = [(i, i ^ 1) for i in range(count)]
    outer = [(i, (i + 1) % count if i % 2 else (i - 1) % count) for i in range(count)]
    return inner, outer


def body(populations, solute, adsorbed, capacity, solid):
    inner_z, outer_z = swaps("ax")
    inner_x, outer_x = swaps("xs")
    own = (4, 16, 256)
    f32 = jnp.float32
    bulk = [message_shape(2)] * 2
    r16, ads16, cap16, solid16, za, zb, *messages = call(
        first_kernel,
        [(FIELDS,) + own, (2,) + own, own, own] + [(112, 256)] * 2 + bulk,
        [
            pltpu.with_memory_space_constraint(x, pltpu.HBM)
            for x in (populations, solute, adsorbed, capacity, solid)
        ],
        specs=[HBM] * 5,
        scratch=[
            pltpu.VMEM((19,) + own, f32),
            pltpu.VMEM((2, 7) + own, f32),
            pltpu.VMEM((2,) + own, f32),
            pltpu.VMEM(own, f32),
            pltpu.VMEM(own, jnp.int32),
            pltpu.SemaphoreType.DMA((4, 5)),
        ],
    )
    zb = lax.ppermute(zb, "ax", outer_z)
    za = lax.ppermute(za, "ax", inner_z)
    messages = [
        lax.ppermute(m, "xs", (outer_x, inner_x)[i % 2]) for i, m in enumerate(messages)
    ]
    token = call(token_kernel, [(8, 128)], [zb], cost=3221225472)[0]
    xb0, xa0 = call(corner_kernel, [message_shape(0)] * 2, [za, zb, token])
    xb0 = lax.ppermute(xb0, "xs", outer_x)
    xa0 = lax.ppermute(xa0, "xs", inner_x)
    rims = [(FIELDS, 4, 8, 256), (2, 4, 8, 256), (4, 8, 256), (4, 8, 256)]
    low, low_ads, low_cap, low_solid = call(
        functools.partial(rim_kernel, 1), rims, messages[:2], cost=1 << 18
    )
    high, high_ads, high_cap, high_solid = call(
        functools.partial(rim_kernel, 2), rims, messages[-2:], cost=1 << 18
    )
    sites = [cap16, solid16, low_cap, low_solid]
    more = [high_cap, high_solid]
    for step in range(1, STEPS):
        first = step == 1
        if first:
            edge_args = [r16, ads16, low, low_ads, xb0, xa0]
            rest_args = edge_args + [high, high_ads]
        else:
            zb = lax.ppermute(zb, "ax", outer_z)
            za = lax.ppermute(za, "ax", inner_z)
            edge_args = rest_args = [r_edge, r_rest, ads_edge, ads_rest]
        edge = STEPS - step
        face = (face_rows(edge - 1), 256)
        r_edge, ads_edge, zb = call(
            functools.partial(edge_kernel, first, edge),
            [(FIELDS, ROWS, 256), (2, ROWS, 256), face],
            edge_args + sites + [zb],
            scratch=[pltpu.VMEM((FIELDS, ROWS, 256), f32)],
            cost=1 << 20,
        )
        r_rest, ads_rest, za = call(
            functools.partial(rest_kernel, first, edge),
            [(FIELDS, 3, ROWS, 256), (2, 3, ROWS, 256), face],
            [r_edge] * first + rest_args + sites + more + [za],
            scratch=[pltpu.VMEM((3, FIELDS, ROWS, 256), f32)],
            cost=3 << 20,
        )
    zb = lax.ppermute(zb, "ax", outer_z)
    za = lax.ppermute(za, "ax", inner_z)
    pops, species, bound = call(
        inner_kernel,
        [(19,) + own, (2, 7) + own, (2,) + own],
        [r_edge, r_rest, ads_edge, ads_rest],
        out_specs=[ANY] * 3,
        scratch=[
            pltpu.VMEM((FIELDS,) + own, f32),
            pltpu.SemaphoreType.DMA((FIELDS, 4)),
            pltpu.SemaphoreType.DMA((2, 4)),
        ],
        cost=3 << 20,
    )
    pops, species = call(
        outer_kernel,
        [(19,) + own, (2, 7) + own],
        [pops, species, za, zb],
        specs=[ANY, ANY, VMEM, VMEM],
        out_specs=[ANY] * 2,
        scratch=[pltpu.SemaphoreType.DMA((FIELDS,))],
        aliases={0: 0, 1: 1},
    )
    return pops, species, bound


def solution(mesh):
    placed = (
        P(None, "ax", "xs", None),
        P(None, None, "ax", "xs", None),
        P(None, "ax", "xs", None),
        P("ax", "xs", None),
        P("ax", "xs", None),
    )
    return jax.shard_map(
        body,
        mesh=mesh,
        in_specs=placed,
        out_specs=(
            P(None, "ax", "xs", None),
            P(None, None, "ax", "xs", None),
            P(None, "ax", "xs", None),
        ),
        check_vma=False,
    )
```

```python
import functools
import jax
import jax.numpy as jnp
import numpy as np
from jax import lax
from jax.experimental import pallas as pl
from jax.experimental.pallas import tpu as pltpu
from jax.sharding import PartitionSpec as P


STEPS = 4
DEPTH = 4
ROWS = 24
VELOCITY = np.array(
    [
        [0, 0, 0],
        [1, 0, 0],
        [-1, 0, 0],
        [0, 1, 0],
        [0, -1, 0],
        [0, 0, 1],
        [0, 0, -1],
        [1, 1, 0],
        [-1, -1, 0],
        [1, -1, 0],
        [-1, 1, 0],
        [1, 0, 1],
        [-1, 0, -1],
        [1, 0, -1],
        [-1, 0, 1],
        [0, 1, 1],
        [0, -1, -1],
        [0, 1, -1],
        [0, -1, 1],
    ]
)
ALL = [tuple(int(c) for c in v) for v in np.concatenate([VELOCITY, VELOCITY[:7], VELOCITY[:7]])]
FIELDS = len(ALL)
UP = [k for k in range(FIELDS) if ALL[k][0] == 1]
DOWN = [k for k in range(FIELDS) if ALL[k][0] == -1]
OMEGA_SOLUTE = (1.0, 0.7)
ON_RATE = (0.5, 0.2)
OFF_RATE = (0.05, 0.1)
VMEM = pl.BlockSpec(memory_space=pltpu.VMEM)
ANY = pl.BlockSpec(memory_space=pl.ANY)
HBM = pl.BlockSpec(memory_space=pltpu.HBM)
MIRROR = [
    19 * (k >= 19) + 7 * (k >= 26)
    + ALL[: 19 if k < 19 else 7].index((-ALL[k][0],) + ALL[k][1:])
    for k in range(FIELDS)
]


def rim_rows(k, side):
    return DEPTH - 1 + side * ALL[k][1]


def message_plan(side, part):
    pieces = []
    for j in range(4):
        for k in range(FIELDS):
            cz = ALL[k][0]
            if part == 0:
                wanted = not 0 <= j - cz < 4
            else:
                wanted = 0 <= j + cz < 4 and (j + cz == 0) == (part == 1)
            if wanted:
                pieces.append(("r", k, j, rim_rows(k, side)))
        if part == (1 if j == 0 else 2):
            pieces += [(n, i, j, 3) for n, i in (("ads", 0), ("ads", 1), ("cap", 0), ("solid", 0))]
    plan, offset = [], 0
    if part == 2:
        offset = message_shape(1)[0]
    for name, k, j, n in pieces:
        plan.append((name, k, j, n, offset))
        offset += n
    return plan, -(-offset // 8) * 8


def message_shape(part):
    return (message_plan(1, part)[1], 256)


def collide(f, adsorbed, capacity, fluid, push):
    out = [None] * FIELDS
    s = {k: f[k] + f[k + 1] for k in range(1, 19, 2)}
    d = {k: f[k] - f[k + 1] for k in range(1, 19, 2)}
    axis = s[1] + s[3] + s[5]
    edge = (s[7] + s[9]) + (s[11] + s[13]) + (s[15] + s[17])
    density = f[0] + axis + edge
    mz = d[1] + d[7] + d[9] + d[11] + d[13]
    mx = d[3] + d[7] - d[9] + d[15] + d[17]
    my = d[5] + d[11] - d[13] + d[15] - d[17]
    inverse = 1.0 / density
    uz, ux, uy = mz * inverse, mx * inverse, my * inverse
    base = 1.0 - 1.5 * (uz * uz + ux * ux + uy * uy)
    even = (1.25 / 36.0) * density
    rest_even = even * base
    square = 4.5 * even
    oz = (2.25 / 36.0) * mz + (push * (0.003 / 36.0)) * density
    ox = (2.25 / 36.0) * mx
    oy = (2.25 / 36.0) * my
    out[0] = jnp.where(fluid, 12.0 * rest_even - 0.25 * f[0], f[0])
    pairs = {
        1: (uz, oz), 3: (ux, ox), 5: (uy, oy),
        7: (uz + ux, oz + ox), 9: (uz - ux, oz - ox),
        11: (uz + uy, oz + oy), 13: (uz - uy, oz - oy),
        15: (ux + uy, ox + oy), 17: (ux - uy, ox - oy),
    }
    for k, (u, o) in pairs.items():
        e = rest_even + square * (u * u)
        if k < 7:
            e, o = e + e, o + o
        a = e - 0.125 * s[k]
        b = o + 0.125 * d[k]
        out[k] = jnp.where(fluid, a + b, f[k + 1])
        out[k + 1] = jnp.where(fluid, a - b, f[k])
    occupied = adsorbed[0] + adsorbed[1]
    free = capacity - occupied
    bound = []
    for kind in range(2):
        g = f[19 + 7 * kind: 26 + 7 * kind]
        total = g[0] + (g[1] + g[2]) + (g[3] + g[4]) + (g[5] + g[6])
        uptake = ON_RATE[kind] * total * free - OFF_RATE[kind] * adsorbed[kind]
        bound.append(jnp.where(fluid, adsorbed[kind] + uptake, adsorbed[kind]))
        omega = OMEGA_SOLUTE[kind]
        moved = total if omega == 1.0 else omega * total
        share = 0.125 * (moved - uptake)
        drift = 0.5 * moved

        def kept(h):
            return 0.0 if omega == 1.0 else (1.0 - omega) * h

        out[19 + 7 * kind] = jnp.where(fluid, kept(g[0]) + (share + share), g[0])
        for j, u in ((1, uz), (3, ux), (5, uy)):
            o = drift * u
            out[19 + 7 * kind + j] = jnp.where(fluid, kept(g[j]) + (share + o), g[j + 1])
            out[19 + 7 * kind + j + 1] = jnp.where(fluid, kept(g[j + 1]) + (share - o), g[j])
    return out, bound


def parity(axis):
    return lax.rem(lax.axis_index(axis), 2)


def turned(p, k):
    return jnp.where(p == 0, k, MIRROR[k]) if MIRROR[k] != k else k


def layer(p, j):
    return jnp.where(p == 0, j, 3 - j)


def first_kernel(
    pop, sol, ads, cap, solid, r_out, ads_out, cap_out, solid_out, za, zb,
    xa, xb, pop_in, sol_in, ads_in, cap_in, solid_in, sems,
):
    sources = {"r": r_out, "ads": ads_out, "cap": cap_out, "solid": solid_out}
    p = parity("ax")
    push = jnp.where(p == 0, 1.0, -1.0)
    copies = []
    for j in range(4):
        z = layer(p, j)
        pairs = [
            (pop.at[:, z], pop_in.at[:, j]),
            (sol.at[:, :, z], sol_in.at[:, :, j]),
            (ads.at[:, z], ads_in.at[:, j]),
            (cap.at[z], cap_in.at[j]),
            (solid.at[z], solid_in.at[j]),
        ]
        copies.append([
            pltpu.make_async_copy(a, b, sems.at[j, i]) for i, (a, b) in enumerate(pairs)
        ])
    for group in copies:
        for copy in group:
            copy.start()
    for j in range(4):
        for copy in copies[j]:
            copy.wait()
        for r in range(0, 16, 8):
            for c in range(0, 256, 128):
                at = (j, slice(r, r + 8), slice(c, c + 128))
                f = [pop_in[(turned(p, k),) + at] for k in range(19)]
                f += [
                    sol_in[(s, turned(p, 19 + 7 * s + k) - 19 - 7 * s) + at]
                    for s in range(2) for k in range(7)
                ]
                cap_out[at] = cap_in[at]
                solid_out[at] = solid_in[at].astype(jnp.float32)
                out, bound = collide(
                    f, [ads_in[(0,) + at], ads_in[(1,) + at]], cap_in[at],
                    solid_in[at] == 0, push,
                )
                for k in range(FIELDS):
                    r_out[(k,) + at] = out[k]
                for s in range(2):
                    ads_out[(s,) + at] = bound[s]

        if j == 0 or j == 3:
            fields, message = (DOWN, zb) if j == 0 else (UP, za)
            for i, k in enumerate(fields):
                message[16 * i:16 * i + 16, :] = turn_columns(k, r_out[k, j])
        for part in (1, 2):
            pack(lambda name, at: sources[name][at], part, xa, xb, (j,))


def pack(read, part, xa, xb, layers=range(4)):
    def fill(side, message):
        for name, k, j, n, offset in message_plan(side, part)[0]:
            if j not in layers:
                continue
            rows = slice(16 - n, 16) if side == 1 else slice(0, n)
            at = (k, j) if name in ("r", "ads") else (j,)
            message[offset:offset + n, :] = read(name, at + (rows, slice(None)))

    q = parity("xs")

    @pl.when(q == 0)
    def _():
        fill(1, xa)
        fill(-1, xb)

    @pl.when(q == 1)
    def _():
        fill(-1, xa)
        fill(1, xb)


def unpack(part, xa, xb, put):
    def empty(side, message):
        for name, k, j, n, offset in message_plan(side, part)[0]:
            put(name, k, j, 8 - n if side == 1 else 0, message[offset:offset + n, :])

    q = parity("xs")

    @pl.when(q == 0)
    def _():
        empty(-1, xa)
        empty(1, xb)

    @pl.when(q == 1)
    def _():
        empty(1, xa)
        empty(-1, xb)


def turn_rows(k, v):
    return pltpu.roll(v, ALL[k][1] % ROWS, 0) if ALL[k][1] else v


def turn_columns(k, v):
    return pltpu.roll(v, ALL[k][2] % 256, 1) if ALL[k][2] else v


def shifted(k, v):
    return turn_columns(k, turn_rows(k, v))


def face_rows(edge):
    return -(-7 * (16 + 2 * edge) // 8) * 8


def send_face(fields, read, message, edge):
    for i, k in enumerate(fields):
        v = shifted(k, read(k))
        message[16 * i:16 * i + 16, :] = v[0:16]
        if edge:
            at = 112 + 2 * edge * i
            message[at:at + edge, :] = v[16:16 + edge]
            message[at + edge:at + 2 * edge, :] = v[24 - edge:24]


def receive_face(k, message, edge, moved):
    i = place_in_face(k)
    moved[0:16, :] = message[16 * i:16 * i + 16, :]
    if edge:
        at = 112 + 2 * edge * i
        moved[16:16 + edge, :] = message[at:at + edge, :]
        moved[24 - edge:24, :] = message[at + edge:at + 2 * edge, :]


def receive_first_faces(j, message, xa0, xb0, moved):
    def put(name, k, layer, low, piece):
        if layer == j:
            moved[k, 16 + low:16 + low + piece.shape[0], :] = piece

    unpack(0, xa0, xb0, put)
    for k in UP if j == 0 else DOWN:
        i = place_in_face(k)
        if ALL[k][1]:
            rows = jnp.concatenate([message[16 * i:16 * i + 16, :], moved[k, 16:24, :]], axis=0)
            moved[k] = turn_rows(k, rows)
        else:
            moved[k, 0:16, :] = message[16 * i:16 * i + 16, :]


def place_in_face(k):
    return (DOWN if ALL[k][0] == 1 else UP).index(MIRROR[k])


def token_kernel(message, token):
    token[...] = message[0:8, 0:128]


def corner_kernel(za, zb, token, xa0, xb0):
    def read(name, at):
        i = 16 * place_in_face(at[0])
        return (zb if at[1] == 0 else za)[i + at[2].start:i + at[2].stop, :]

    pack(read, 0, xa0, xb0)


def rim_kernel(part, xa, xb, rim, rim_ads, rim_cap, rim_solid):
    arrays = {"r": rim, "ads": rim_ads, "cap": rim_cap, "solid": rim_solid}

    def put(name, k, j, low, piece):
        at = (k, j) if name in ("r", "ads") else (j,)
        arrays[name][at + (slice(low, low + piece.shape[0]), slice(None))] = piece

    unpack(part, xa, xb, put)


class Split:
    def __init__(self, own, first, second):
        self.own, self.first, self.second = own, first, second

    def rim(self, k, j):
        cz = 0 if k is None or self.own.shape[0] == 2 else ALL[k][0]
        return self.first if j + cz == 0 else self.second

    def whole(self, k, j):
        return jnp.concatenate([self.own[k, j], self.rim(k, j)[k, j]], axis=0)

    def block(self, k, j, r, cols):
        at = (j,) if k is None else (k, j)
        if r < 16:
            return self.own[at + (slice(r, r + 8), cols)]
        return self.rim(k, j)[at + (slice(0, 8), cols)]


class Layers:
    def __init__(self, edge, rest):
        self.edge, self.rest = edge, rest

    def whole(self, k, j):
        return self.edge[k] if j == 0 else self.rest[k, j - 1]

    def block(self, k, j, r, cols):
        if j == 0:
            return self.edge[k, r:r + 8, cols]
        return self.rest[k, j - 1, r:r + 8, cols]


def step_layer(j, state, ads, cap, solid, message, corners, edge, push, moved, store):
    through = []
    if corners and j in (0, 3):
        receive_first_faces(j, message, *corners, moved)
    for k in range(FIELDS):
        source = j - ALL[k][0]
        if source == -1 or source == 4:
            if not corners:
                receive_face(k, message, edge, moved.at[k])
        elif ALL[k][1:] == (0, 0):
            through.append(k)
        else:
            moved[k] = shifted(k, state.whole(k, source))
    for r in range(0, ROWS, 8):
        for c in range(0, 256, 128):
            cols = slice(c, c + 128)
            f = [
                state.block(k, j - ALL[k][0], r, cols) if k in through
                else moved[k, r:r + 8, cols]
                for k in range(FIELDS)
            ]
            out, bound = collide(
                f,
                [ads.block(s, j, r, cols) for s in range(2)],
                cap.block(None, j, r, cols),
                solid.block(None, j, r, cols) == 0.0,
                push,
            )
            store(r, cols, out, bound)


def edge_kernel(first, edge, *refs):
    if first:
        r16, ads16, rim, rim_ads, xa0, xb0 = refs[:6]
        state, ads = Split(r16, rim, None), Split(ads16, rim_ads, None)
        corners = (xa0, xb0)
        refs = refs[6:]
    else:
        state, ads, corners = Layers(*refs[:2]), Layers(*refs[2:4]), ()
        refs = refs[4:]
    cap16, solid16, rim_cap, rim_solid, zb, r_out, ads_out, zb_out, moved = refs
    cap, solid = Split(cap16, rim_cap, None), Split(solid16, rim_solid, None)
    push = jnp.where(parity("ax") == 0, 1.0, -1.0)

    def store(r, cols, out, bound):
        for k in range(FIELDS):
            r_out[k, r:r + 8, cols] = out[k]
        for s in range(2):
            ads_out[s, r:r + 8, cols] = bound[s]

    step_layer(0, state, ads, cap, solid, zb, corners, edge, push, moved, store)
    send_face(DOWN, lambda k: r_out[k], zb_out, edge - 1)


def rest_kernel(first, edge, *refs):
    refs = list(refs)
    if first:
        edge_ref, r16, ads16, low, low_ads, xa0, xb0, high, high_ads = refs[:9]
        state, ads = Split(r16, low, high), Split(ads16, low_ads, high_ads)
        corners = (xa0, xb0)
        refs = refs[9:]
    else:
        state, ads, corners = Layers(*refs[:2]), Layers(*refs[2:4]), ()
        refs = refs[4:]
    cap16, solid16, low_cap, low_solid, high_cap, high_solid = refs[:6]
    cap, solid = Split(cap16, low_cap, high_cap), Split(solid16, low_solid, high_solid)
    za, r_out, ads_out, za_out, moved = refs[6:]
    push = jnp.where(parity("ax") == 0, 1.0, -1.0)
    for j in range(1, 4):
        def store(r, cols, out, bound):
            for k in range(FIELDS):
                r_out[k, j - 1, r:r + 8, cols] = out[k]
            for s in range(2):
                ads_out[s, j - 1, r:r + 8, cols] = bound[s]

        step_layer(j, state, ads, cap, solid, za, corners, edge, push, moved.at[j - 1], store)
    send_face(UP, lambda k: r_out[k, 2], za_out, edge - 1)


def place(p, k, z, pop, sol):
    if k < 19:
        return pop.at[turned(p, k), z]
    s = (k - 19) // 7
    return sol.at[s, turned(p, k) - 19 - 7 * s, z]


def inner_kernel(r_edge, r_rest, ads_edge, ads_rest, pop, sol, ads, stage, sems, ads_sems):
    p = parity("ax")
    state = Layers(r_edge, r_rest)
    copies = []
    for s in range(2):
        for j in range(4):
            source = ads_edge.at[s, 0:16] if j == 0 else ads_rest.at[s, j - 1, 0:16]
            copies.append(
                pltpu.make_async_copy(source, ads.at[s, layer(p, j)], ads_sems.at[s, j])
            )
            copies[-1].start()
    for j in range(4):
        for k in range(FIELDS):
            source = j - ALL[k][0]
            if 0 <= source < 4:
                stage[k, j] = shifted(k, state.whole(k, source))[0:16]
                copies.append(
                    pltpu.make_async_copy(
                        stage.at[k, j], place(p, k, layer(p, j), pop, sol), sems.at[k, j]
                    )
                )
                copies[-1].start()
    for copy in copies:
        copy.wait()


def outer_kernel(pop_in, sol_in, za, zb, pop, sol, sems):
    p = parity("ax")
    copies = []
    for fields, message, j in ((UP, zb, 0), (DOWN, za, 3)):
        for k in fields:
            i = place_in_face(k)
            copies.append(
                pltpu.make_async_copy(
                    message.at[16 * i:16 * i + 16],
                    place(p, k, layer(p, j), pop, sol),
                    sems.at[k],
                )
            )
            copies[-1].start()
    for copy in copies:
        copy.wait()


def call(kernel, outs, args, specs=None, out_specs=None, scratch=(), cost=0, aliases=None):
    return pl.pallas_call(
        kernel,
        out_shape=[jax.ShapeDtypeStruct(s, jnp.float32) for s in outs],
        in_specs=specs or [VMEM] * len(args),
        out_specs=out_specs or [VMEM] * len(outs),
        scratch_shapes=list(scratch),
        input_output_aliases=aliases or {},
        cost_estimate=pl.CostEstimate(
            flops=cost, bytes_accessed=cost // 4, transcendentals=0
        ),
        compiler_params=pltpu.CompilerParams(vmem_limit_bytes=16 << 20),
    )(*args)


def swaps(axis):
    count = lax.axis_size(axis)
    inner = [(i, i ^ 1) for i in range(count)]
    outer = [(i, (i + 1) % count if i % 2 else (i - 1) % count) for i in range(count)]
    return inner, outer


def body(populations, solute, adsorbed, capacity, solid):
    inner_z, outer_z = swaps("ax")
    inner_x, outer_x = swaps("xs")
    own = (4, 16, 256)
    f32 = jnp.float32
    bulk = [message_shape(2)] * 2
    r16, ads16, cap16, solid16, za, zb, *messages = call(
        first_kernel,
        [(FIELDS,) + own, (2,) + own, own, own] + [(112, 256)] * 2 + bulk,
        [
            pltpu.with_memory_space_constraint(x, pltpu.HBM)
            for x in (populations, solute, adsorbed, capacity, solid)
        ],
        specs=[HBM] * 5,
        scratch=[
            pltpu.VMEM((19,) + own, f32),
            pltpu.VMEM((2, 7) + own, f32),
            pltpu.VMEM((2,) + own, f32),
            pltpu.VMEM(own, f32),
            pltpu.VMEM(own, jnp.int32),
            pltpu.SemaphoreType.DMA((4, 5)),
        ],
    )
    zb = lax.ppermute(zb, "ax", outer_z)
    za = lax.ppermute(za, "ax", inner_z)
    messages = [
        lax.ppermute(m, "xs", (inner_x, outer_x)[i % 2]) for i, m in enumerate(messages)
    ]
    token = call(token_kernel, [(8, 128)], [zb], cost=3221225472)[0]
    xa0, xb0 = call(corner_kernel, [message_shape(0)] * 2, [za, zb, token])
    xb0 = lax.ppermute(xb0, "xs", outer_x)
    xa0 = lax.ppermute(xa0, "xs", inner_x)
    rims = [(FIELDS, 4, 8, 256), (2, 4, 8, 256), (4, 8, 256), (4, 8, 256)]
    low, low_ads, low_cap, low_solid = call(
        functools.partial(rim_kernel, 1), rims, messages[:2], cost=1 << 18
    )
    high, high_ads, high_cap, high_solid = call(
        functools.partial(rim_kernel, 2), rims, messages[-2:], cost=1 << 18
    )
    sites = [cap16, solid16, low_cap, low_solid]
    more = [high_cap, high_solid]
    for step in range(1, STEPS):
        first = step == 1
        if first:
            edge_args = [r16, ads16, low, low_ads, xa0, xb0]
            rest_args = edge_args + [high, high_ads]
        else:
            zb = lax.ppermute(zb, "ax", outer_z)
            za = lax.ppermute(za, "ax", inner_z)
            edge_args = rest_args = [r_edge, r_rest, ads_edge, ads_rest]
        edge = STEPS - step
        face = (face_rows(edge - 1), 256)
        r_edge, ads_edge, zb = call(
            functools.partial(edge_kernel, first, edge),
            [(FIELDS, ROWS, 256), (2, ROWS, 256), face],
            edge_args + sites + [zb],
            scratch=[pltpu.VMEM((FIELDS, ROWS, 256), f32)],
            cost=1 << 20,
        )
        r_rest, ads_rest, za = call(
            functools.partial(rest_kernel, first, edge),
            [(FIELDS, 3, ROWS, 256), (2, 3, ROWS, 256), face],
            [r_edge] * first + rest_args + sites + more + [za],
            scratch=[pltpu.VMEM((3, FIELDS, ROWS, 256), f32)],
            cost=3 << 20,
        )
    zb = lax.ppermute(zb, "ax", outer_z)
    za = lax.ppermute(za, "ax", inner_z)
    pops, species, bound = call(
        inner_kernel,
        [(19,) + own, (2, 7) + own, (2,) + own],
        [r_edge, r_rest, ads_edge, ads_rest],
        out_specs=[ANY] * 3,
        scratch=[
            pltpu.VMEM((FIELDS,) + own, f32),
            pltpu.SemaphoreType.DMA((FIELDS, 4)),
            pltpu.SemaphoreType.DMA((2, 4)),
        ],
        cost=3 << 20,
    )
    pops, species = call(
        outer_kernel,
        [(19,) + own, (2, 7) + own],
        [pops, species, za, zb],
        specs=[ANY, ANY, VMEM, VMEM],
        out_specs=[ANY] * 2,
        scratch=[pltpu.SemaphoreType.DMA((FIELDS,))],
        aliases={0: 0, 1: 1},
    )
    return pops, species, bound


def solution(mesh):
    placed = (
        P(None, "ax", "xs", None),
        P(None, None, "ax", "xs", None),
        P(None, "ax", "xs", None),
        P("ax", "xs", None),
        P("ax", "xs", None),
    )
    return jax.shard_map(
        body,
        mesh=mesh,
        in_specs=placed,
        out_specs=(
            P(None, "ax", "xs", None),
            P(None, None, "ax", "xs", None),
            P(None, "ax", "xs", None),
        ),
        check_vma=False,
    )
```
